32 devices in a mesh: ctx: 16 (over z, y, core), wt: 2 (over x).
Axes of the slice: x: 2, y: 2, z: 4, core: 2. Of those that a mesh axis runs over, the one named last changes fastest.
Arguments:
- inputs: bfloat16 [6144, 1472], P('ctx'), may hold values from -24 to 24
- delete_mask: bfloat16 [6144], P('ctx'), may hold values from -4 to 0
- lengths: int32 [6], replicated, may hold values from 1024 to 1024, as said below
- dealing: int32 [6144], replicated, may hold values from 0 to 6143, as said below
- w_query: bfloat16 [1472, 384], P(None, 'wt'), may hold values from -0.0390625 to 0.0390625
- w_key: bfloat16 [1472, 384], P(None, 'wt'), may hold values from -0.15625 to 0.15625
- w_value: bfloat16 [1472, 384], P(None, 'wt'), may hold values from -0.15625 to 0.15625
- w_output: bfloat16 [384, 1472], P('wt'), may hold values from -0.875 to 0.875
- bias_table: float32 [32, 6], P(None, 'wt'), may hold values from -4 to 4
- norm_attn: float32 [1472], replicated, may hold values from 0.5 to 1.5
- w_gate: bfloat16 [1472, 3584], P(None, 'wt'), may hold values from -0.15625 to 0.15625
- w_up: bfloat16 [1472, 3584], P(None, 'wt'), may hold values from -0.15625 to 0.15625
- w_down: bfloat16 [3584, 1472], P('wt'), may hold values from -0.09375 to 0.09375
- norm_ffn: float32 [1472], replicated, may hold values from 0.5 to 1.5
- out_grad: bfloat16 [6144, 1472], P('ctx'), may hold values from -6 to 6
Outputs:
- output: bfloat16 [6144, 1472], P('ctx')
- input_grad: bfloat16 [6144, 1472], P('ctx')
- mask_grad: bfloat16 [6144], P('ctx')
- grad_query: float32 [1472, 384], P('ctx', 'wt')
- grad_key: float32 [1472, 384], P('ctx', 'wt')
- grad_value: float32 [1472, 384], P('ctx', 'wt')
- grad_output: float32 [384, 1472], P('wt', 'ctx')
- grad_table: float32 [32, 6], P(None, 'wt')
- grad_norm_attn: float32 [1472], P('ctx')
- grad_gate: float32 [1472, 3584], P('ctx', 'wt')
- grad_up: float32 [1472, 3584], P('ctx', 'wt')
- grad_down: float32 [3584, 1472], P('wt', 'ctx')
- grad_norm_ffn: float32 [1472], P('ctx')
- root_means: float32 [3], replicated
The draws below stay inside these ranges and needn't reach their ends.
Inputs may be any that keep to these rules, and one draw needn't show every extreme that they name: Sequence s takes the tokens from the sum of the earlier lengths on; the lengths sum to 6144; in every draw one sequence has exactly 1024 tokens and one exactly 1024. `dealing`: A permutation of the tokens. The 384 dealt slots of each index of ctx take exactly 24 tokens from each block of 384 consecutive tokens, the blocks in order, so slot c * 384 + b * 24 + m holds a token of block b.
All inputs are finite; a program needn't handle non-finite values.
Results may differ from the reference program's by a relative error of at most 0.018.
Values may be sent and summed in bfloat16 or wider, within the bound.
A program may use at most 256 MiB of HBM per device.

```python
import jax
import jax.numpy as jnp
from jax import lax

D = 1472
HEADS = 6
HD = 64
FF = 3584
NB = 32
TOK_DEV = 384
MIN_LEN = 1024
TOKENS = 6144
SEQS = 6


def draw_lengths(key, part):
    couples = SEQS // 2
    average = TOKENS // SEQS
    excess = average - MIN_LEN
    key_share, key_order = jax.random.split(key)
    shares = jax.random.randint(key_share, (couples,), 0, 2 * excess + 1).astype(jnp.int32)
    shares = shares.at[0].set(2 * excess)
    longer = MIN_LEN + shares
    shorter = MIN_LEN + 2 * excess - shares
    joined = jnp.concatenate([longer, shorter]).astype(jnp.int32)
    shuffle = jax.random.permutation(key_order, SEQS)
    return joined[shuffle].astype(jnp.int32)


def deal_table(key):
    dealt_key = jax.random.fold_in(key, 11)
    blocks_all = TOKENS // TOK_DEV
    quota_each = TOK_DEV // blocks_all
    streams = jax.random.split(dealt_key, blocks_all)
    shuffled = jax.vmap(lambda stream: jax.random.permutation(stream, TOK_DEV))(streams).astype(jnp.int32)
    shuffled = shuffled + (jnp.arange(blocks_all, dtype=jnp.int32) * TOK_DEV)[:, None]
    grouped = shuffled.reshape(blocks_all, blocks_all, quota_each)
    return jnp.transpose(grouped, (1, 0, 2)).reshape(TOKENS).astype(jnp.int32)


def draw_dealing(key, part):
    return deal_table(key)


def draw_inputs(key, part):
    dealt = deal_table(key)
    blocks_all = TOKENS // TOK_DEV
    slot_owner = (jnp.arange(TOKENS, dtype=jnp.int32) // TOK_DEV).astype(jnp.int32)
    owner = jnp.zeros((TOKENS,), jnp.int32).at[dealt].set(slot_owner)
    fraction = owner.astype(jnp.float32) / (blocks_all - 1)
    value_key = jax.random.fold_in(key, 23)
    base = jnp.clip(jax.random.normal(value_key, (TOKENS, D), jnp.float32), -6.0, 6.0)
    scale = jnp.exp(fraction * jnp.log(3.0))
    return (base * scale[:, None]).astype(jnp.bfloat16)


def shard_levels(own_key, shape, shards, smallest, top_value):
    factor_of = 1.0
    for dim, blocks in shards:
        draws = jax.random.uniform(jax.random.fold_in(jax.random.fold_in(own_key, 6), dim), (blocks,), jnp.float32, smallest / len(shards), top_value / len(shards))
        factor_of = factor_of * jnp.repeat(jnp.exp(draws), shape[dim] // blocks).reshape((-1,) + (1,) * (len(shape) - 1 - dim))
    return factor_of


def scatter_about(key, extent, scale, bound, pieces=(), held_as=jnp.bfloat16):
    gain = shard_levels(key, extent, pieces, -0.22, 0.18) if pieces else 1.0
    result = jax.random.normal(key, extent, jnp.float32) * scale * gain
    return jnp.minimum(jnp.maximum(result, -bound), bound).astype(held_as)


def setup_inputs(seed: int = 0) -> dict:
    keys = jax.random.split(jax.random.key(seed), 16)
    inputs = draw_inputs(jax.random.fold_in(keys[15], 71), 0)
    delete_mask = jnp.clip(-4.0 + 4.0 * jax.random.uniform(keys[1], (TOKENS,), jnp.float32) ** shard_levels(keys[1], (TOKENS,), ((0, 16),), -0.2, 0.2), -4.0, 0.0).astype(jnp.bfloat16)
    lengths = draw_lengths(jax.random.fold_in(keys[15], 71), 0)
    dealing = draw_dealing(jax.random.fold_in(keys[15], 71), 0)
    w_query = scatter_about(keys[4], (D, HEADS * HD), (16 * D) ** -0.5, 0.0390625, ((1, 2),))
    w_key = scatter_about(keys[5], (D, HEADS * HD), D ** -0.5, 0.15625, ((1, 2),))
    w_value = scatter_about(keys[6], (D, HEADS * HD), D ** -0.5, 0.15625, ((1, 2),))
    w_output = scatter_about(keys[7], (HEADS * HD, D), (HEADS * HD // 8) ** -0.5, 0.875, ((0, 2),))
    bias_table = scatter_about(keys[8], (NB, HEADS), 1.0, 4.0, ((1, 2),), jnp.float32)
    norm_attn = jnp.clip(1.0 + 0.1 * jax.random.normal(keys[9], (D,), jnp.float32), 0.5, 1.5)
    w_gate = scatter_about(keys[10], (D, FF), D ** -0.5, 0.15625, ((1, 2),))
    w_up = scatter_about(keys[11], (D, FF), D ** -0.5, 0.15625, ((1, 2),))
    w_down = scatter_about(keys[12], (FF, D), FF ** -0.5, 0.09375, ((0, 2),))
    norm_ffn = jnp.clip(1.0 + 0.1 * jax.random.normal(keys[13], (D,), jnp.float32), 0.5, 1.5)
    out_grad = scatter_about(keys[14], (TOKENS, D), 1.0, 6.0, ((0, 16),))
    return dict(inputs=inputs, delete_mask=delete_mask, lengths=lengths, dealing=dealing, w_query=w_query, w_key=w_key, w_value=w_value, w_output=w_output, bias_table=bias_table, norm_attn=norm_attn, w_gate=w_gate, w_up=w_up, w_down=w_down, norm_ffn=norm_ffn, out_grad=out_grad)


@jax.custom_vjp
def low(v):
    return lax.optimization_barrier(v.astype(jnp.bfloat16)).astype(jnp.float32)

@jax.custom_vjp
def low_back(v):
    return v

def low_keep(v):
    return (low(v), None)

def low_pass(kept, grad):
    return (grad,)

def back_keep(v):
    return (v, None)

def back_low(kept, grad):
    return (low(grad),)
low.defvjp(low_keep, low_pass)
low_back.defvjp(back_keep, back_low)
THRESHOLDS = (1, 2, 3, 4, 5, 6, 7, 8, 12, 16, 23, 32, 46, 64, 91)
MASKED = -1e+30
EPSILON = 1e-06

def bucket_of(offset):
    distance = jnp.abs(offset)
    bucket_sum = (offset > 0).astype(jnp.int32) * 16
    for threshold in THRESHOLDS:
        bucket_sum = bucket_sum + (distance >= threshold).astype(jnp.int32)
    return bucket_sum.astype(jnp.int32)

def places(initial, lengths):
    starts = (jnp.cumsum(lengths) - lengths).astype(jnp.int32)
    inside = initial[:, None] >= starts[None, :]
    sequence = lax.optimization_barrier(jnp.sum(inside.astype(jnp.int32), axis=1)) - 1
    opening = lax.optimization_barrier(jnp.max(jnp.where(inside, starts[None, :], 0), axis=1))
    return (sequence.astype(jnp.int32), (initial - opening).astype(jnp.int32))

def product(left_side, right_side):
    return jnp.dot(left_side, right_side, precision=lax.Precision.HIGHEST)

def rms_norm(values_in, gain_in):
    inverse = lax.rsqrt(lax.optimization_barrier(jnp.mean(values_in * values_in, axis=-1, keepdims=True)) + EPSILON)
    return values_in * inverse * gain_in

def attend(queries, keys_in, values_in, mask_in, table_in, seq_all, pos_all):
    tokens_all = queries.shape[0]
    rows_block = 256
    block_count = tokens_all // rows_block
    key_heads = keys_in.reshape(tokens_all, HEADS, HD)
    value_heads = values_in.reshape(tokens_all, HEADS, HD)

    def one_block(block_in):
        query_part, seq_part, pos_part = block_in
        raw_score = low_back(jnp.einsum('qhd,khd->hqk', query_part, key_heads, precision=lax.Precision.HIGHEST))
        bucket = bucket_of(pos_all[None, :] - pos_part[:, None])
        added_terms = jnp.transpose(table_in[bucket], (2, 0, 1)) + mask_in[None, None, :]
        same_seq = seq_all[None, :] == seq_part[:, None]
        scores = jnp.where(same_seq[None], raw_score + added_terms, MASKED)
        probs_here = jax.nn.softmax(scores, axis=-1)
        return jnp.einsum('hqk,khd->qhd', low(probs_here), value_heads, precision=lax.Precision.HIGHEST)
    block_out = lax.map(jax.checkpoint(one_block), (queries.reshape(block_count, rows_block, HEADS, HD), seq_all.reshape(block_count, rows_block), pos_all.reshape(block_count, rows_block)))
    return block_out.reshape(tokens_all, HEADS * HD)

def reference(inputs, delete_mask, lengths, dealing, w_query, w_key, w_value, w_output, bias_table, norm_attn, w_gate, w_up, w_down, norm_ffn, out_grad):
    tokens_all = inputs.shape[0]
    model_width = inputs.shape[1]
    seq_all, pos_all = places(jnp.arange(tokens_all, dtype=jnp.int32), lengths)

    def forward(stream_in, mask_in, query_w, key_w, value_w, output_w, table_in, gain_one, gate_w, up_w, down_w, gain_two):
        hidden_one = low(rms_norm(stream_in, gain_one))
        queries = low_back(low(product(hidden_one, query_w)))
        keys_in = low_back(low(product(hidden_one, key_w)))
        values_in = low_back(low(product(hidden_one, value_w)))
        attended = low_back(low(attend(queries, keys_in, values_in, mask_in, table_in, seq_all, pos_all)))
        branch_attn = low_back(product(attended, output_w))
        stream_mid = stream_in + branch_attn
        hidden_two = low(rms_norm(stream_mid, gain_two))
        gate_value = low_back(product(hidden_two, gate_w))
        up_value = low_back(product(hidden_two, up_w))
        inner_low = low(jax.nn.gelu(gate_value, approximate=True) * up_value)
        branch_ffn = product(inner_low, down_w)
        stream_out = stream_mid + branch_ffn
        scale_all = 1.0 / (tokens_all * model_width)
        squares = jnp.stack([jnp.sum(stream_out * stream_out), jnp.sum(branch_attn * branch_attn), jnp.sum(branch_ffn * branch_ffn)])
        return (stream_out, jnp.sqrt(squares * scale_all))
    stream_out, pull, root_means = jax.vjp(forward, inputs.astype(jnp.float32), delete_mask.astype(jnp.float32), w_query.astype(jnp.float32), w_key.astype(jnp.float32), w_value.astype(jnp.float32), w_output.astype(jnp.float32), bias_table.astype(jnp.float32), norm_attn.astype(jnp.float32), w_gate.astype(jnp.float32), w_up.astype(jnp.float32), w_down.astype(jnp.float32), norm_ffn.astype(jnp.float32), has_aux=True)
    grads = pull(out_grad.astype(jnp.float32))
    return (stream_out.astype(jnp.bfloat16), grads[0].astype(jnp.bfloat16), grads[1][dealing].astype(jnp.bfloat16), grads[2], grads[3], grads[4], grads[5], grads[6], grads[7], grads[8], grads[9], grads[10], grads[11], root_means)
```

```python
from functools import partial

import jax
import jax.numpy as jnp
from jax import lax
from jax.experimental import pallas as pl
from jax.experimental.pallas import tpu as pltpu
from jax.sharding import PartitionSpec as P

HD = 64
MIN_LEN = 1024
CHUNK = 128
THRESHOLDS = (1, 2, 3, 4, 5, 6, 7, 8, 12, 16, 23, 32, 46, 64, 91)
MASKED = -1e30
EPSILON = 1e-06
F32 = jnp.float32
BF16 = jnp.bfloat16


def bucket_of(offset):
    distance = jnp.abs(offset)
    bucket_sum = (offset > 0).astype(jnp.int32) * 16
    for threshold in THRESHOLDS:
        bucket_sum = bucket_sum + (distance >= threshold).astype(jnp.int32)
    return bucket_sum


def running_starts(lengths):
    count = lengths.shape[0]
    order = jnp.arange(count, dtype=jnp.int32)
    earlier = order[None, :] < order[:, None]
    return jnp.sum(jnp.where(earlier, lengths[None, :], 0), axis=1)


def places(initial, lengths):
    starts = running_starts(lengths)
    inside = initial[:, None] >= starts[None, :]
    sequence = jnp.sum(inside.astype(jnp.int32), axis=1) - 1
    opening = jnp.max(jnp.where(inside, starts[None, :], 0), axis=1)
    return (sequence, initial - opening)


def dot(left, right):
    return jnp.dot(left, right, preferred_element_type=F32)


def mat_t(left, right):
    return lax.dot_general(left, right, (((1,), (1,)), ((), ())), preferred_element_type=F32)


def t_mat(left, right):
    return lax.dot_general(left, right, (((0,), (0,)), ((), ())), preferred_element_type=F32)


def norm_back(grad_in, normed, inverse, gain_in):
    scaled = grad_in * gain_in
    return inverse * (scaled - normed * jnp.mean(scaled * normed, axis=-1, keepdims=True))


def pair_terms(table_here, query_seq, query_pos, key_seq, key_pos, key_mask):
    bucket = bucket_of(key_pos[None, :] - query_pos[:, None])
    bucket_ids = jnp.arange(table_here.shape[0], dtype=jnp.int32)
    chosen = bucket[None, :, :, None] == bucket_ids[None, None, None, :]
    table_heads = jnp.transpose(table_here)[:, None, None, :]
    added_terms = jnp.sum(jnp.where(chosen, table_heads, 0.0), axis=-1)
    added_terms = added_terms + key_mask.astype(F32)[None, None, :]
    same_seq = key_seq[None, :] == query_seq[:, None]
    return (added_terms, same_seq, chosen)


def score_block(query_heads, key_heads, added_terms, same_seq):
    raw_score = jnp.einsum("qhd,khd->hqk", query_heads, key_heads, preferred_element_type=F32)
    return jnp.where(same_seq[None], raw_score + added_terms, MASKED)


class General:
    def __init__(self, q, k, v, mask, lengths, table):
        self.tok = q.shape[0]
        self.cols = q.shape[1]
        heads = self.cols // HD
        self.table = table
        n = lax.axis_size("ctx")
        self.all = self.tok * n
        rows = 2 * self.tok
        blocks = self.all // rows
        seq_all, pos_all = places(jnp.arange(self.all, dtype=jnp.int32), lengths)
        first = lax.axis_index("ctx") * self.tok
        self.q_seq = lax.dynamic_slice_in_dim(seq_all, first, self.tok)
        self.q_pos = lax.dynamic_slice_in_dim(pos_all, first, self.tok)
        self.q = q.reshape(self.tok, heads, HD)
        self.blocks = (
            lax.all_gather(k, "ctx", axis=0, tiled=True).reshape(blocks, rows, heads, HD),
            lax.all_gather(v, "ctx", axis=0, tiled=True).reshape(blocks, rows, heads, HD),
            seq_all.reshape(blocks, rows),
            pos_all.reshape(blocks, rows),
            lax.all_gather(mask, "ctx", axis=0, tiled=True).reshape(blocks, rows),
        )
        self.heads = heads

    def forward(self):
        def top_step(state, block):
            top, total = state
            k, _, seq, pos, mask = block
            added, same, _ = pair_terms(self.table, self.q_seq, self.q_pos, seq, pos, mask)
            scores = score_block(self.q, k, added, same)
            new_top = jnp.maximum(top, jnp.max(scores, axis=-1))
            total = total * jnp.exp(top - new_top) + jnp.sum(
                jnp.exp(scores - new_top[..., None]), axis=-1
            )
            return ((new_top, total), None)

        def value_step(out, block):
            high, low = out
            k, v, seq, pos, mask = block
            added, same, _ = pair_terms(self.table, self.q_seq, self.q_pos, seq, pos, mask)
            probs = jnp.exp(score_block(self.q, k, added, same) - self.lse[..., None])
            probs_high = probs.astype(BF16)
            rest = (probs - probs_high.astype(F32)).astype(BF16)
            high = high + jnp.einsum("hqk,khd->qhd", probs_high, v, preferred_element_type=F32)
            low = low + jnp.einsum("hqk,khd->qhd", rest, v, preferred_element_type=F32)
            return ((high, low), None)

        start = (
            jnp.full((self.heads, self.tok), MASKED, F32),
            jnp.zeros((self.heads, self.tok), F32),
        )
        (top, total), _ = lax.scan(top_step, start, self.blocks)
        self.lse = top + jnp.log(total)
        self.zero = jnp.zeros((self.tok, self.heads, HD), F32)
        (high, low), _ = lax.scan(value_step, (self.zero, self.zero), self.blocks)
        self.exact = high + low
        return high.reshape(self.tok, self.cols).astype(BF16)

    def backward(self, do):
        grad = do.reshape(self.tok, self.heads, HD)
        delta = jnp.transpose(jnp.sum(grad.astype(F32) * self.exact, axis=-1))

        def step(state, block):
            q_acc, table_acc = state
            k, v, seq, pos, mask = block
            added, same, chosen = pair_terms(self.table, self.q_seq, self.q_pos, seq, pos, mask)
            probs = jnp.exp(score_block(self.q, k, added, same) - self.lse[..., None])
            dp = jnp.einsum("qhd,khd->hqk", grad, v, preferred_element_type=F32)
            ds = probs * (dp - delta[..., None])
            low = ds.astype(BF16)
            q_acc = q_acc + jnp.einsum("hqk,khd->qhd", low, k, preferred_element_type=F32)
            sums = jnp.sum(jnp.where(chosen, ds[..., None], 0.0), axis=(1, 2))
            emitted = (
                jnp.einsum("hqk,qhd->khd", low, self.q, preferred_element_type=F32),
                jnp.einsum("hqk,qhd->khd", probs.astype(BF16), grad, preferred_element_type=F32),
                jnp.sum(ds, axis=(0, 1)),
            )
            return ((q_acc, table_acc + jnp.transpose(sums)), emitted)

        start = (self.zero, jnp.zeros((self.table.shape[0], self.heads), F32))
        (q_acc, table_acc), (dk, dv, dm) = lax.scan(step, start, self.blocks)
        dk = lax.psum_scatter(
            dk.reshape(self.all, self.cols), "ctx", scatter_dimension=0, tiled=True
        )
        dv = lax.psum_scatter(
            dv.reshape(self.all, self.cols), "ctx", scatter_dimension=0, tiled=True
        )
        dq = q_acc.reshape(self.tok, self.cols)
        return (dq.astype(BF16), dk.astype(BF16), dv.astype(BF16), table_acc, dm.reshape(self.all))


def head_lanes(shape, head, value_order):
    lane = lax.broadcasted_iota(jnp.int32, shape, 1) // HD
    place = (head + 2 if head < 2 else 1) if value_order else head
    return lane == place


def chunk_place(ctx, i, chunks, halo):
    g = ctx * chunks + i
    per = MIN_LEN // CHUNK
    within = lax.rem(g, per)
    window = (g - within) * CHUNK - (ctx - halo) * chunks * CHUNK
    return within, pl.multiple_of(window, CHUNK)


def bias_fill(near_ref, bias_ref, heads):
    per = MIN_LEN // CHUNK
    for h in range(heads):
        strip = near_ref[h : h + 1, :]
        wide = jnp.broadcast_to(strip, (CHUNK, 512))
        tile = pltpu.roll(wide, 512 - 127, 1, stride=1, stride_axis=0)
        bias_ref[h, :, pl.ds(0, (per - 2) * CHUNK)] = jnp.broadcast_to(
            strip[:, 0:1], (CHUNK, (per - 2) * CHUNK)
        )
        bias_ref[h, :, pl.ds((per - 2) * CHUNK, 3 * CHUNK)] = tile[:, : 3 * CHUNK]
        bias_ref[h, :, pl.ds((per + 1) * CHUNK, (per - 2) * CHUNK)] = jnp.broadcast_to(
            strip[:, 510:511], (CHUNK, (per - 2) * CHUNK)
        )


def forward_kernel(halo, heads, q_ref, kv_ref, mask_ref, near_ref, o_ref, lse_ref, bias_ref):
    ctx = lax.axis_index("ctx")
    chunks = q_ref.shape[0] // CHUNK
    per = MIN_LEN // CHUNK
    bias_fill(near_ref, bias_ref, heads)
    for i in range(chunks):
        within, window = chunk_place(ctx, i, chunks, halo)
        q = q_ref[i * CHUNK : (i + 1) * CHUNK, :]
        keys = kv_ref[pl.ds(window, MIN_LEN), 0:256]
        values = kv_ref[pl.ds(window, MIN_LEN), 128:384]
        mask = mask_ref[:, pl.ds(window, MIN_LEN)]
        out = jnp.zeros((CHUNK, 256), F32)
        lse = jnp.zeros((CHUNK, CHUNK), F32)
        for h in range(heads):
            s = mat_t(jnp.where(head_lanes(q.shape, h, False), q, jnp.zeros_like(q)), keys)
            start = pl.multiple_of((per - 1 - within) * CHUNK, CHUNK)
            s = s + bias_ref[h, :, pl.ds(start, MIN_LEN)] + mask
            top = jnp.max(s, axis=1, keepdims=True)
            e = jnp.exp(s - top)
            total = jnp.sum(e, axis=1, keepdims=True)
            p = (e * (1.0 / total)).astype(BF16)
            out = jnp.where(head_lanes(out.shape, h, True), dot(p, values), out)
            lane = lax.broadcasted_iota(jnp.int32, lse.shape, 1)
            lse = jnp.where(lane == h, top + jnp.log(total), lse)
        o_ref[i * CHUNK : (i + 1) * CHUNK, :] = out.astype(BF16)
        lse_ref[i * CHUNK : (i + 1) * CHUNK, :] = lse


def fold_diagonals(tile):
    rows = tile.shape[0]
    width = tile.shape[1]
    while rows > 1:
        rows //= 2
        tile = tile[:rows] + pltpu.roll(tile[rows:], width - rows, 1)
    return tile


def backward_kernel(
    halo,
    heads,
    q_ref,
    kv_ref,
    mask_ref,
    near_ref,
    do_ref,
    lse_ref,
    dq_ref,
    dkv_ref,
    dmask_ref,
    dnear_ref,
    dfar_ref,
    bias_ref,
    acc_ref,
    ds_ref,
    tile_ref,
):
    ctx = lax.axis_index("ctx")
    chunks = q_ref.shape[0] // CHUNK
    per = MIN_LEN // CHUNK
    bias_fill(near_ref, bias_ref, heads)
    acc_ref[...] = jnp.zeros_like(acc_ref)
    dmask_ref[...] = jnp.zeros_like(dmask_ref)
    tile_ref[...] = jnp.zeros_like(tile_ref)
    ds_ref[:, 0:CHUNK] = jnp.zeros((CHUNK, CHUNK), F32)
    ds_ref[:, MIN_LEN + CHUNK :] = jnp.zeros((CHUNK, CHUNK), F32)
    far = [jnp.zeros((1, MIN_LEN), F32) for _ in range(2 * heads)]
    for i in range(chunks):
        within, window = chunk_place(ctx, i, chunks, halo)
        rows = slice(i * CHUNK, (i + 1) * CHUNK)
        q = q_ref[rows, :]
        do = do_ref[rows, :]
        lse = lse_ref[rows, :]
        keys = kv_ref[pl.ds(window, MIN_LEN), 0:256]
        values = kv_ref[pl.ds(window, MIN_LEN), 128:384]
        mask = mask_ref[:, pl.ds(window, MIN_LEN)]
        column = lax.broadcasted_iota(jnp.int32, (1, MIN_LEN), 1) // CHUNK
        dq = jnp.zeros((CHUNK, 256), F32)
        dmask = jnp.zeros((1, MIN_LEN), F32)
        dkeys = jnp.zeros((MIN_LEN, 256), F32)
        dvalues = jnp.zeros((MIN_LEN, 256), F32)
        for h in range(heads):
            qm = jnp.where(head_lanes(q.shape, h, False), q, jnp.zeros_like(q))
            dom = jnp.where(head_lanes(do.shape, h, True), do, jnp.zeros_like(do))
            start = pl.multiple_of((per - 1 - within) * CHUNK, CHUNK)
            s = mat_t(qm, keys) + bias_ref[h, :, pl.ds(start, MIN_LEN)] + mask
            p = jnp.exp(s - lse[:, h : h + 1])
            dp = mat_t(dom, values)
            delta = jnp.sum(p * dp, axis=1, keepdims=True)
            ds = p * (dp - delta)
            low = ds.astype(BF16)
            dq = jnp.where(head_lanes(dq.shape, h, False), dot(low, keys), dq)
            dkeys = dkeys + t_mat(low, qm)
            dvalues = dvalues + t_mat(p.astype(BF16), dom)
            sums = jnp.sum(ds, axis=0, keepdims=True)
            dmask = dmask + sums
            far[2 * h] = far[2 * h] + jnp.where(column < within - 1, sums, 0.0)
            far[2 * h + 1] = far[2 * h + 1] + jnp.where(column > within + 1, sums, 0.0)
            ds_ref[:, CHUNK : CHUNK + MIN_LEN] = ds
            near = pl.multiple_of(within * CHUNK, CHUNK)
            tile_ref[h, :, 0 : 3 * CHUNK] += ds_ref[:, pl.ds(near, 3 * CHUNK)]
        dq_ref[rows, :] = dq.astype(BF16)
        dmask_ref[:, pl.ds(window, MIN_LEN)] += dmask
        acc_ref[pl.ds(window, MIN_LEN), 0:256] += dkeys
        acc_ref[pl.ds(window, MIN_LEN), 128:384] += dvalues
    dkv_ref[...] = acc_ref[...].astype(BF16)
    for h in range(heads):
        dnear_ref[h : h + 1, :] = fold_diagonals(tile_ref[h])
        for side in range(2):
            dfar_ref[2 * h + side : 2 * h + side + 1, :] = jnp.broadcast_to(
                jnp.sum(far[2 * h + side], axis=1, keepdims=True), (1, CHUNK)
            )


def needed_blocks(ctx, tok):
    low = (ctx * tok) // MIN_LEN * MIN_LEN
    high = ((ctx + 1) * tok + MIN_LEN - 1) // MIN_LEN * MIN_LEN
    return low // tok, -(-high // tok)


def whole_spec():
    return pl.BlockSpec(memory_space=pltpu.VMEM)


class Even:
    def __init__(self, q, kv, mask, table):
        self.tok = q.shape[0]
        self.heads = table.shape[1]
        n = lax.axis_size("ctx")
        self.count = n
        self.ctx = lax.axis_index("ctx")
        spans = [needed_blocks(c, self.tok) for c in range(n)]
        self.shifts = sorted(
            {j - c for c in range(n) for j in range(max(spans[c][0], 0), min(spans[c][1], n))}
            - {0},
            key=abs,
        )
        self.pairs = {
            s: [(c + s, c) for c in range(n) if spans[c][0] <= c + s < min(spans[c][1], n)]
            for s in self.shifts
        }
        self.halo = max(abs(s) for s in self.shifts)
        self.q = q
        blocks = {0: kv}
        for s in self.shifts:
            blocks[s] = lax.ppermute(kv, "ctx", self.pairs[s])
        zero = jnp.zeros_like(kv)
        self.kv = jnp.concatenate(
            [blocks.get(s, zero) for s in range(-self.halo, self.halo + 1)], axis=0
        )
        pad = self.halo * self.tok
        padded = jnp.pad(lax.all_gather(mask, "ctx", axis=0, tiled=True).astype(F32), (pad, pad))
        self.window = (2 * self.halo + 1) * self.tok
        self.mask = lax.dynamic_slice_in_dim(padded, self.ctx * self.tok, self.window)[None, :]
        offsets = jnp.arange(512, dtype=jnp.int32) - 255
        ids = jnp.arange(table.shape[0], dtype=jnp.int32)
        self.chosen = bucket_of(offsets)[:, None] == ids[None, :]
        self.near = jnp.sum(jnp.where(self.chosen[None], jnp.transpose(table)[:, None, :], 0.0), -1)

    def forward(self):
        o, self.lse = pl.pallas_call(
            partial(forward_kernel, self.halo, self.heads),
            out_shape=(
                jax.ShapeDtypeStruct((self.tok, 256), BF16),
                jax.ShapeDtypeStruct((self.tok, CHUNK), F32),
            ),
            in_specs=[whole_spec()] * 4,
            out_specs=(whole_spec(), whole_spec()),
            scratch_shapes=[pltpu.VMEM((self.heads, CHUNK, 2 * MIN_LEN - CHUNK), F32)],
            compiler_params=pltpu.CompilerParams(vmem_limit_bytes=40 << 20),
            name="attend",
        )(self.q, self.kv, self.mask, self.near)
        return jnp.concatenate([o[:, 128:], o[:, 64:128]], axis=1)

    def backward(self, do):
        spread = jnp.concatenate([jnp.zeros((self.tok, 64), BF16), do[:, 128:], do[:, :128]], 1)
        dq, dkv, dmask, dnear, dfar = pl.pallas_call(
            partial(backward_kernel, self.halo, self.heads),
            out_shape=(
                jax.ShapeDtypeStruct((self.tok, 256), BF16),
                jax.ShapeDtypeStruct((self.window, 384), BF16),
                jax.ShapeDtypeStruct((1, self.window), F32),
                jax.ShapeDtypeStruct((self.heads, 512), F32),
                jax.ShapeDtypeStruct((2 * self.heads, CHUNK), F32),
            ),
            in_specs=[whole_spec()] * 6,
            out_specs=(whole_spec(),) * 5,
            scratch_shapes=[
                pltpu.VMEM((self.heads, CHUNK, 2 * MIN_LEN - CHUNK), F32),
                pltpu.VMEM((self.window, 384), F32),
                pltpu.VMEM((CHUNK, MIN_LEN + 2 * CHUNK), F32),
                pltpu.VMEM((self.heads, CHUNK, 512), F32),
            ],
            compiler_params=pltpu.CompilerParams(vmem_limit_bytes=40 << 20),
            name="attend_back",
        )(self.q, self.kv, self.mask, self.near, spread, self.lse)
        tok = self.tok
        total = dkv[self.halo * tok : (self.halo + 1) * tok].astype(F32)
        for s in self.shifts:
            part = dkv[(self.halo + s) * tok : (self.halo + s + 1) * tok]
            back = lax.ppermute(part, "ctx", [(b, a) for a, b in self.pairs[s]])
            total = total + back.astype(F32)
        total = total.astype(BF16)
        dk = total[:, :192]
        dv = jnp.concatenate([total[:, 256:], total[:, 192:256]], axis=1)
        offsets = jnp.arange(512, dtype=jnp.int32)
        offsets = jnp.where(offsets < 3 * CHUNK, offsets, offsets - 512) - CHUNK
        ids = jnp.arange(self.chosen.shape[1], dtype=jnp.int32)
        chosen = bucket_of(offsets)[:, None] == ids[None, :]
        table = jnp.sum(jnp.where(chosen[None], dnear[:, :, None], 0.0), axis=1)
        table = table + jnp.where(ids == 15, 1.0, 0.0)[None] * dfar[0::2, :1]
        table = table + jnp.where(ids == 31, 1.0, 0.0)[None] * dfar[1::2, :1]
        pad = self.halo * tok
        spread_mask = lax.dynamic_update_slice_in_dim(
            jnp.zeros((self.count * tok + 2 * pad,), F32), dmask[0], self.ctx * tok, 0
        )
        return dq[:, :192], dk, dv, jnp.transpose(table), spread_mask[pad : pad + self.count * tok]


class Halving:
    def __init__(self, width):
        self.n = lax.axis_size("ctx")
        self.bits = self.n.bit_length() - 1
        self.own = width // self.n
        self.rows = -(-self.own // 16) * 16
        places = [int(format(b, f"0{self.bits}b")[::-1], 2) for b in range(self.n)]
        order = jnp.asarray(places, jnp.int32)
        owner = jnp.bitwise_xor(order, lax.axis_index("ctx"))
        inner = jnp.arange(self.rows, dtype=jnp.int32)
        source = jnp.where(inner < self.own, owner[:, None] * self.own + inner, -1).reshape(-1)
        features = jnp.arange(width, dtype=jnp.int32)
        self.select = (features[:, None] == source[None, :]).astype(BF16)

    def arrange(self, x):
        return dot(x, self.select).astype(BF16)

    def scatter(self, left, right):
        half = left.shape[1] // 2
        send = t_mat(left[:, half:], right).astype(BF16)
        keep = t_mat(left[:, :half], right).astype(BF16)
        for bit in range(self.bits):
            pairs = [(i, i ^ (1 << bit)) for i in range(self.n)]
            got = lax.ppermute(send, "ctx", pairs)
            half = half // 2
            if bit == self.bits - 1:
                return keep[: self.own].astype(F32) + got[: self.own].astype(F32)
            send = (keep[half:].astype(F32) + got[half:].astype(F32)).astype(BF16)
            keep = (keep[:half].astype(F32) + got[:half].astype(F32)).astype(BF16)


def local(
    inputs,
    delete_mask,
    lengths,
    dealing,
    w_query,
    w_key,
    w_value,
    w_output,
    bias_table,
    norm_attn,
    w_gate,
    w_up,
    w_down,
    norm_ffn,
    out_grad,
):
    tok = inputs.shape[0]
    width = inputs.shape[1]
    n = lax.axis_size("ctx")
    ctx = lax.axis_index("ctx")
    wt = lax.axis_index("wt")
    tokens_all = tok * n
    cols = w_query.shape[1]
    even = (
        tokens_all == MIN_LEN * lengths.shape[0]
        and tok % CHUNK == 0
        and cols == 3 * HD
        and lax.axis_size("wt") == 2
    )
    swap = [(0, 1), (1, 0)]

    def other(x):
        return lax.ppermute(x, "wt", swap)

    sums = Halving(width)
    stream_in = inputs.astype(F32)
    inverse_one = lax.rsqrt(jnp.mean(stream_in * stream_in, axis=-1, keepdims=True) + EPSILON)
    normed_one = stream_in * inverse_one
    hidden_one = (normed_one * norm_attn).astype(BF16)
    if even:
        joined = jnp.concatenate([w_key, w_value[:, 128:], w_value[:, :128]], axis=1)
        queries = dot(hidden_one, jnp.pad(w_query, ((0, 0), (0, 64)))).astype(BF16)
        attention = Even(queries, dot(hidden_one, joined).astype(BF16), delete_mask, bias_table)
    else:
        attention = General(
            dot(hidden_one, w_query).astype(BF16),
            dot(hidden_one, w_key).astype(BF16),
            dot(hidden_one, w_value).astype(BF16),
            delete_mask,
            lengths,
            bias_table,
        )
    w_output_other = other(w_output)
    arranged_grad = sums.arrange(out_grad)
    arranged_one = sums.arrange(hidden_one)
    inner_grad = mat_t(out_grad, w_down)
    attended = attention.forward()
    branch_attn = dot(attended, w_output) + dot(other(attended), w_output_other)
    stream_mid = stream_in + branch_attn
    inverse_two = lax.rsqrt(jnp.mean(stream_mid * stream_mid, axis=-1, keepdims=True) + EPSILON)
    normed_two = stream_mid * inverse_two
    hidden_two = (normed_two * norm_ffn).astype(BF16)
    gate_value = dot(hidden_two, w_gate)
    up_value = dot(hidden_two, w_up)

    def gated_unit(gate_in, up_in):
        return jax.nn.gelu(gate_in, approximate=True) * up_in

    activated, gated_pull = jax.vjp(gated_unit, gate_value, up_value)
    inner_low = activated.astype(BF16)
    down_part = sums.scatter(arranged_grad, inner_low)
    gate_grad, up_grad = gated_pull(inner_grad)
    gate_low = gate_grad.astype(BF16)
    up_low = up_grad.astype(BF16)
    back_part = (mat_t(gate_low, w_gate) + mat_t(up_low, w_up)).astype(BF16)
    hidden_two_grad = back_part.astype(F32) + other(back_part).astype(F32)
    arranged_two = sums.arrange(hidden_two)
    gate_part = sums.scatter(arranged_two, gate_low)
    up_part = sums.scatter(arranged_two, up_low)
    gain_two_grad = jnp.sum(hidden_two_grad * normed_two, axis=0)
    stream_mid_grad = out_grad.astype(F32) + norm_back(
        hidden_two_grad, normed_two, inverse_two, norm_ffn
    )
    attn_grad_low = stream_mid_grad.astype(BF16)
    attended_grad = mat_t(attn_grad_low, w_output).astype(BF16)
    output_part = sums.scatter(sums.arrange(attn_grad_low), attended)
    ffn_part = dot(inner_low, w_down).astype(BF16)
    branch_ffn = ffn_part.astype(F32) + other(ffn_part).astype(F32)
    stream_out = stream_mid + branch_ffn
    squares = jnp.stack(
        [
            jnp.sum(stream_out * stream_out),
            jnp.sum(branch_attn * branch_attn),
            jnp.sum(branch_ffn * branch_ffn),
        ]
    )
    dq, dk, dv, table_acc, dmask = attention.backward(attended_grad)
    projections = jnp.concatenate([dq, dk, dv], axis=1)
    projection_part = sums.scatter(arranged_one, projections)
    w_all = jnp.concatenate([w_query, w_key, w_value], axis=1)
    one_part = mat_t(projections, w_all).astype(BF16)
    hidden_one_grad = one_part.astype(F32) + other(one_part).astype(F32)
    gain_one_grad = jnp.sum(hidden_one_grad * normed_one, axis=0)
    input_grad = stream_mid_grad + norm_back(hidden_one_grad, normed_one, inverse_one, norm_attn)
    heads = table_acc.shape[1]
    flat = table_acc.reshape(-1)
    table_slots = jnp.where(
        jnp.arange(2)[:, None] == wt, jnp.broadcast_to(flat, (2, flat.shape[0])), 0.0
    ).reshape(-1)
    small = jnp.concatenate(
        [
            dmask,
            table_slots,
            0.5 * gain_one_grad,
            0.5 * gain_two_grad,
            0.5 * squares,
        ]
    )
    small = lax.psum(small, ("ctx", "wt"))
    mask_all = small[:tokens_all].reshape(n, 1, tok)
    base = tokens_all
    table_grad = lax.dynamic_slice_in_dim(small, base + wt * flat.shape[0], flat.shape[0])
    table_grad = table_grad.reshape(-1, heads)
    base += 2 * flat.shape[0]
    own = width // n
    gain_one = lax.dynamic_slice_in_dim(small, base + ctx * own, own)
    gain_two = lax.dynamic_slice_in_dim(small, base + width + ctx * own, own)
    square_sum = small[base + 2 * width :]
    root_means = jnp.sqrt(square_sum / (tokens_all * width))
    quota = tok // n
    slots = lax.dynamic_slice_in_dim(dealing, ctx * tok, tok).reshape(n, quota, 1)
    inside = slots - (jnp.arange(n, dtype=jnp.int32) * tok)[:, None, None]
    chosen = inside == jnp.arange(tok, dtype=jnp.int32)[None, None, :]
    mask_grad = jnp.sum(jnp.where(chosen, mask_all, 0.0), axis=-1).reshape(tok)
    return (
        stream_out.astype(BF16),
        input_grad.astype(BF16),
        mask_grad.astype(BF16),
        projection_part[:, :cols],
        projection_part[:, cols : 2 * cols],
        projection_part[:, 2 * cols :],
        jnp.transpose(output_part),
        table_grad,
        gain_one,
        gate_part,
        up_part,
        jnp.transpose(down_part),
        gain_two,
        root_means,
    )


def solution(mesh):
    return jax.shard_map(
        local,
        mesh=mesh,
        in_specs=(
            P("ctx", None),
            P("ctx"),
            P(),
            P(),
            P(None, "wt"),
            P(None, "wt"),
            P(None, "wt"),
            P("wt", None),
            P(None, "wt"),
            P(),
            P(None, "wt"),
            P(None, "wt"),
            P("wt", None),
            P(),
            P("ctx", None),
        ),
        out_specs=(
            P("ctx", None),
            P("ctx", None),
            P("ctx"),
            P("ctx", "wt"),
            P("ctx", "wt"),
            P("ctx", "wt"),
            P("wt", "ctx"),
            P(None, "wt"),
            P("ctx"),
            P("ctx", "wt"),
            P("ctx", "wt"),
            P("wt", "ctx"),
            P("ctx"),
            P(),
        ),
        check_vma=False,
    )
```

```python
from functools import partial

import jax
import jax.numpy as jnp
from jax import lax
from jax.experimental import pallas as pl
from jax.experimental.pallas import tpu as pltpu
from jax.sharding import PartitionSpec as P

HD = 64
MIN_LEN = 1024
CHUNK = 128
THRESHOLDS = (1, 2, 3, 4, 5, 6, 7, 8, 12, 16, 23, 32, 46, 64, 91)
MASKED = -1e30
EPSILON = 1e-06
F32 = jnp.float32
BF16 = jnp.bfloat16


def bucket_of(offset):
    distance = jnp.abs(offset)
    bucket_sum = (offset > 0).astype(jnp.int32) * 16
    for threshold in THRESHOLDS:
        bucket_sum = bucket_sum + (distance >= threshold).astype(jnp.int32)
    return bucket_sum


def running_starts(lengths):
    count = lengths.shape[0]
    order = jnp.arange(count, dtype=jnp.int32)
    earlier = order[None, :] < order[:, None]
    return jnp.sum(jnp.where(earlier, lengths[None, :], 0), axis=1)


def places(initial, lengths):
    starts = running_starts(lengths)
    inside = initial[:, None] >= starts[None, :]
    sequence = jnp.sum(inside.astype(jnp.int32), axis=1) - 1
    opening = jnp.max(jnp.where(inside, starts[None, :], 0), axis=1)
    return (sequence, initial - opening)


def dot(left, right):
    return jnp.dot(left, right, preferred_element_type=F32)


def mat_t(left, right):
    return lax.dot_general(left, right, (((1,), (1,)), ((), ())), preferred_element_type=F32)


def t_mat(left, right):
    return lax.dot_general(left, right, (((0,), (0,)), ((), ())), preferred_element_type=F32)


def norm_back(grad_in, normed, inverse, gain_in):
    scaled = grad_in * gain_in
    return inverse * (scaled - normed * jnp.mean(scaled * normed, axis=-1, keepdims=True))


def pair_terms(table_here, query_seq, query_pos, key_seq, key_pos, key_mask):
    bucket = bucket_of(key_pos[None, :] - query_pos[:, None])
    bucket_ids = jnp.arange(table_here.shape[0], dtype=jnp.int32)
    chosen = bucket[None, :, :, None] == bucket_ids[None, None, None, :]
    table_heads = jnp.transpose(table_here)[:, None, None, :]
    added_terms = jnp.sum(jnp.where(chosen, table_heads, 0.0), axis=-1)
    added_terms = added_terms + key_mask.astype(F32)[None, None, :]
    same_seq = key_seq[None, :] == query_seq[:, None]
    return (added_terms, same_seq, chosen)


def score_block(query_heads, key_heads, added_terms, same_seq):
    raw_score = jnp.einsum("qhd,khd->hqk", query_heads, key_heads, preferred_element_type=F32)
    return jnp.where(same_seq[None], raw_score + added_terms, MASKED)


class General:
    def __init__(self, q, k, v, mask, lengths, table):
        self.tok = q.shape[0]
        self.cols = q.shape[1]
        heads = self.cols // HD
        self.table = table
        n = lax.axis_size("ctx")
        self.all = self.tok * n
        rows = 2 * self.tok
        blocks = self.all // rows
        seq_all, pos_all = places(jnp.arange(self.all, dtype=jnp.int32), lengths)
        first = lax.axis_index("ctx") * self.tok
        self.q_seq = lax.dynamic_slice_in_dim(seq_all, first, self.tok)
        self.q_pos = lax.dynamic_slice_in_dim(pos_all, first, self.tok)
        self.q = q.reshape(self.tok, heads, HD)
        self.blocks = (
            lax.all_gather(k, "ctx", axis=0, tiled=True).reshape(blocks, rows, heads, HD),
            lax.all_gather(v, "ctx", axis=0, tiled=True).reshape(blocks, rows, heads, HD),
            seq_all.reshape(blocks, rows),
            pos_all.reshape(blocks, rows),
            lax.all_gather(mask, "ctx", axis=0, tiled=True).reshape(blocks, rows),
        )
        self.heads = heads

    def forward(self):
        def top_step(state, block):
            top, total = state
            k, _, seq, pos, mask = block
            added, same, _ = pair_terms(self.table, self.q_seq, self.q_pos, seq, pos, mask)
            scores = score_block(self.q, k, added, same)
            new_top = jnp.maximum(top, jnp.max(scores, axis=-1))
            total = total * jnp.exp(top - new_top) + jnp.sum(
                jnp.exp(scores - new_top[..., None]), axis=-1
            )
            return ((new_top, total), None)

        def value_step(out, block):
            high, low = out
            k, v, seq, pos, mask = block
            added, same, _ = pair_terms(self.table, self.q_seq, self.q_pos, seq, pos, mask)
            probs = jnp.exp(score_block(self.q, k, added, same) - self.lse[..., None])
            probs_high = probs.astype(BF16)
            rest = (probs - probs_high.astype(F32)).astype(BF16)
            high = high + jnp.einsum("hqk,khd->qhd", probs_high, v, preferred_element_type=F32)
            low = low + jnp.einsum("hqk,khd->qhd", rest, v, preferred_element_type=F32)
            return ((high, low), None)

        start = (
            jnp.full((self.heads, self.tok), MASKED, F32),
            jnp.zeros((self.heads, self.tok), F32),
        )
        (top, total), _ = lax.scan(top_step, start, self.blocks)
        self.lse = top + jnp.log(total)
        self.zero = jnp.zeros((self.tok, self.heads, HD), F32)
        (high, low), _ = lax.scan(value_step, (self.zero, self.zero), self.blocks)
        self.exact = high + low
        return high.reshape(self.tok, self.cols).astype(BF16)

    def backward(self, do):
        grad = do.reshape(self.tok, self.heads, HD)
        delta = jnp.transpose(jnp.sum(grad.astype(F32) * self.exact, axis=-1))

        def step(state, block):
            q_acc, table_acc = state
            k, v, seq, pos, mask = block
            added, same, chosen = pair_terms(self.table, self.q_seq, self.q_pos, seq, pos, mask)
            probs = jnp.exp(score_block(self.q, k, added, same) - self.lse[..., None])
            dp = jnp.einsum("qhd,khd->hqk", grad, v, preferred_element_type=F32)
            ds = probs * (dp - delta[..., None])
            low = ds.astype(BF16)
            q_acc = q_acc + jnp.einsum("hqk,khd->qhd", low, k, preferred_element_type=F32)
            sums = jnp.sum(jnp.where(chosen, ds[..., None], 0.0), axis=(1, 2))
            emitted = (
                jnp.einsum("hqk,qhd->khd", low, self.q, preferred_element_type=F32),
                jnp.einsum("hqk,qhd->khd", probs.astype(BF16), grad, preferred_element_type=F32),
                jnp.sum(ds, axis=(0, 1)),
            )
            return ((q_acc, table_acc + jnp.transpose(sums)), emitted)

        start = (self.zero, jnp.zeros((self.table.shape[0], self.heads), F32))
        (q_acc, table_acc), (dk, dv, dm) = lax.scan(step, start, self.blocks)
        dk = lax.psum_scatter(
            dk.reshape(self.all, self.cols), "ctx", scatter_dimension=0, tiled=True
        )
        dv = lax.psum_scatter(
            dv.reshape(self.all, self.cols), "ctx", scatter_dimension=0, tiled=True
        )
        dq = q_acc.reshape(self.tok, self.cols)
        return (dq.astype(BF16), dk.astype(BF16), dv.astype(BF16), table_acc, dm.reshape(self.all))


class Halving:
    def __init__(self, width):
        self.n = lax.axis_size("ctx")
        self.bits = self.n.bit_length() - 1
        self.own = width // self.n
        self.rows = -(-self.own // 16) * 16
        places = [int(format(b, f"0{self.bits}b")[::-1], 2) for b in range(self.n)]
        order = jnp.asarray(places, jnp.int32)
        owner = jnp.bitwise_xor(order, lax.axis_index("ctx"))
        inner = jnp.arange(self.rows, dtype=jnp.int32)
        source = jnp.where(inner < self.own, owner[:, None] * self.own + inner, -1).reshape(-1)
        features = jnp.arange(width, dtype=jnp.int32)
        self.select = (features[:, None] == source[None, :]).astype(BF16)

    def arrange(self, x):
        return dot(x, self.select).astype(BF16)

    def scatter(self, left, right):
        half = left.shape[1] // 2
        send = t_mat(left[:, half:], right).astype(BF16)
        keep = t_mat(left[:, :half], right).astype(BF16)
        for bit in range(self.bits):
            pairs = [(i, i ^ (1 << bit)) for i in range(self.n)]
            got = lax.ppermute(send, "ctx", pairs)
            half = half // 2
            if bit == self.bits - 1:
                return keep[: self.own].astype(F32) + got[: self.own].astype(F32)
            send = (keep[half:].astype(F32) + got[half:].astype(F32)).astype(BF16)
            keep = (keep[:half].astype(F32) + got[:half].astype(F32)).astype(BF16)


def general(
    inputs,
    delete_mask,
    lengths,
    dealing,
    w_query,
    w_key,
    w_value,
    w_output,
    bias_table,
    norm_attn,
    w_gate,
    w_up,
    w_down,
    norm_ffn,
    out_grad,
):
    tok = inputs.shape[0]
    width = inputs.shape[1]
    n = lax.axis_size("ctx")
    ctx = lax.axis_index("ctx")
    wt = lax.axis_index("wt")
    tokens_all = tok * n
    cols = w_query.shape[1]
    swap = [(0, 1), (1, 0)]

    def other(x):
        return lax.ppermute(x, "wt", swap)

    sums = Halving(width)
    stream_in = inputs.astype(F32)
    inverse_one = lax.rsqrt(jnp.mean(stream_in * stream_in, axis=-1, keepdims=True) + EPSILON)
    normed_one = stream_in * inverse_one
    hidden_one = (normed_one * norm_attn).astype(BF16)
    attention = General(
        dot(hidden_one, w_query).astype(BF16),
        dot(hidden_one, w_key).astype(BF16),
        dot(hidden_one, w_value).astype(BF16),
        delete_mask,
        lengths,
        bias_table,
    )
    w_output_other = other(w_output)
    arranged_grad = sums.arrange(out_grad)
    arranged_one = sums.arrange(hidden_one)
    inner_grad = mat_t(out_grad, w_down)
    attended = attention.forward()
    branch_attn = dot(attended, w_output) + dot(other(attended), w_output_other)
    stream_mid = stream_in + branch_attn
    inverse_two = lax.rsqrt(jnp.mean(stream_mid * stream_mid, axis=-1, keepdims=True) + EPSILON)
    normed_two = stream_mid * inverse_two
    hidden_two = (normed_two * norm_ffn).astype(BF16)
    gate_value = dot(hidden_two, w_gate)
    up_value = dot(hidden_two, w_up)

    def gated_unit(gate_in, up_in):
        return jax.nn.gelu(gate_in, approximate=True) * up_in

    activated, gated_pull = jax.vjp(gated_unit, gate_value, up_value)
    inner_low = activated.astype(BF16)
    down_part = sums.scatter(arranged_grad, inner_low)
    gate_grad, up_grad = gated_pull(inner_grad)
    gate_low = gate_grad.astype(BF16)
    up_low = up_grad.astype(BF16)
    back_part = (mat_t(gate_low, w_gate) + mat_t(up_low, w_up)).astype(BF16)
    hidden_two_grad = back_part.astype(F32) + other(back_part).astype(F32)
    arranged_two = sums.arrange(hidden_two)
    gate_part = sums.scatter(arranged_two, gate_low)
    up_part = sums.scatter(arranged_two, up_low)
    gain_two_grad = jnp.sum(hidden_two_grad * normed_two, axis=0)
    stream_mid_grad = out_grad.astype(F32) + norm_back(
        hidden_two_grad, normed_two, inverse_two, norm_ffn
    )
    attn_grad_low = stream_mid_grad.astype(BF16)
    attended_grad = mat_t(attn_grad_low, w_output).astype(BF16)
    output_part = sums.scatter(sums.arrange(attn_grad_low), attended)
    ffn_part = dot(inner_low, w_down).astype(BF16)
    branch_ffn = ffn_part.astype(F32) + other(ffn_part).astype(F32)
    stream_out = stream_mid + branch_ffn
    squares = jnp.stack(
        [
            jnp.sum(stream_out * stream_out),
            jnp.sum(branch_attn * branch_attn),
            jnp.sum(branch_ffn * branch_ffn),
        ]
    )
    dq, dk, dv, table_acc, dmask = attention.backward(attended_grad)
    projections = jnp.concatenate([dq, dk, dv], axis=1)
    projection_part = sums.scatter(arranged_one, projections)
    w_all = jnp.concatenate([w_query, w_key, w_value], axis=1)
    one_part = mat_t(projections, w_all).astype(BF16)
    hidden_one_grad = one_part.astype(F32) + other(one_part).astype(F32)
    gain_one_grad = jnp.sum(hidden_one_grad * normed_one, axis=0)
    input_grad = stream_mid_grad + norm_back(hidden_one_grad, normed_one, inverse_one, norm_attn)
    heads = table_acc.shape[1]
    flat = table_acc.reshape(-1)
    table_slots = jnp.where(
        jnp.arange(2)[:, None] == wt, jnp.broadcast_to(flat, (2, flat.shape[0])), 0.0
    ).reshape(-1)
    small = jnp.concatenate(
        [
            dmask,
            table_slots,
            0.5 * gain_one_grad,
            0.5 * gain_two_grad,
            0.5 * squares,
        ]
    )
    small = lax.psum(small, ("ctx", "wt"))
    mask_all = small[:tokens_all].reshape(n, 1, tok)
    base = tokens_all
    table_grad = lax.dynamic_slice_in_dim(small, base + wt * flat.shape[0], flat.shape[0])
    table_grad = table_grad.reshape(-1, heads)
    base += 2 * flat.shape[0]
    own = width // n
    gain_one = lax.dynamic_slice_in_dim(small, base + ctx * own, own)
    gain_two = lax.dynamic_slice_in_dim(small, base + width + ctx * own, own)
    square_sum = small[base + 2 * width :]
    root_means = jnp.sqrt(square_sum / (tokens_all * width))
    quota = tok // n
    slots = lax.dynamic_slice_in_dim(dealing, ctx * tok, tok).reshape(n, quota, 1)
    inside = slots - (jnp.arange(n, dtype=jnp.int32) * tok)[:, None, None]
    chosen = inside == jnp.arange(tok, dtype=jnp.int32)[None, None, :]
    mask_grad = jnp.sum(jnp.where(chosen, mask_all, 0.0), axis=-1).reshape(tok)
    return (
        stream_out.astype(BF16),
        input_grad.astype(BF16),
        mask_grad.astype(BF16),
        projection_part[:, :cols],
        projection_part[:, cols : 2 * cols],
        projection_part[:, 2 * cols :],
        jnp.transpose(output_part),
        table_grad,
        gain_one,
        gate_part,
        up_part,
        jnp.transpose(down_part),
        gain_two,
        root_means,
    )


PER = MIN_LEN // CHUNK
SHIFTS = (-3, -2, -1, 1, 2, 3)
TILE = 256
MESH = pl.DeviceIdType.MESH
GELU = 0.7978845608028654
CUBIC = 0.044715


def iota(shape, axis):
    return lax.broadcasted_iota(jnp.int32, shape, axis)


def head_lanes(shape, head, value_order):
    place = (head + 2 if head < 2 else 1) if value_order else head
    return iota(shape, 1) // HD == place


def holds(device, sequence):
    first = (sequence * PER) // 3
    last = (sequence * PER + PER - 1) // 3
    return jnp.logical_and(device >= first, device <= last)


def inside(device):
    return jnp.logical_and(device >= 0, device < 16)


def flip(index, bit):
    return index + bit * (1 - 2 * ((index // bit) % 2))


def multiple(value, of):
    return value if isinstance(value, int) else pl.multiple_of(value, of)


def copy_to(src, dst, send, recv, ctx, wt):
    return pltpu.make_async_remote_copy(
        src_ref=src,
        dst_ref=dst,
        send_sem=send,
        recv_sem=recv,
        device_id=(ctx, wt),
        device_id_type=MESH,
    )


def row_blocks(width, size=CHUNK):
    return [slice(k, min(k + size, width)) for k in range(0, width, size)]


def announce(ctx, wt, bits):
    barrier = pltpu.get_barrier_semaphore()
    count = 1 + len(bits)
    pl.semaphore_signal(barrier, inc=1, device_id=(ctx, 1 - wt), device_id_type=MESH)
    for bit in bits:
        pl.semaphore_signal(
            barrier, inc=1, device_id=(flip(ctx, bit), wt), device_id_type=MESH
        )
    for shift in SHIFTS:
        peer = ctx + shift

        @pl.when(inside(peer))
        def _():
            pl.semaphore_signal(barrier, inc=1, device_id=(peer, wt), device_id_type=MESH)

        count = count + inside(peer).astype(jnp.int32)
    return barrier, count


def gain_of(norms_ref, rows, which):
    return jnp.transpose(norms_ref[:, rows])[:, which : which + 1]


def arrange(src_ref, lhs_ref, half_ref, ctx, own):
    rows = lhs_ref.shape[0] // 8

    def block(b, dst_ref, side):
        owner = ((ctx % 2) + side) % 2
        for k in range(1, 4):
            mine = (ctx // (1 << k)) % 2
            turn = (b // (8 >> k)) % 2
            owner = owner + (mine + turn - 2 * mine * turn) * (1 << k)
        start = owner * own
        base = pl.multiple_of((start // 8) * 8, 8)
        tall = src_ref[pl.ds(base, rows + 8), :]
        tall = jnp.where(start % 8 == 0, tall[:rows], tall[4 : rows + 4])
        dst_ref[pl.ds(pl.multiple_of(b * rows, rows), rows), 0 : src_ref.shape[1]] = tall.astype(
            BF16
        )

    def both(b, carry):
        block(b, lhs_ref, 0)
        block(b, half_ref, 1)
        return carry

    lax.fori_loop(0, 8, both, 0)


def near_tiles(near_ref, tiles_ref):
    for h in range(3):
        wide = jnp.broadcast_to(near_ref[h : h + 1, :], (CHUNK, 512))
        tile = pltpu.roll(wide, 512 - 127, 1, stride=1, stride_axis=0)
        tiles_ref[h] = tile[:, : 3 * CHUNK]


def bias_row(near_ref, tiles_ref, row_ref, h, within):
    lane = iota((1, MIN_LEN + 2 * CHUNK), 1) // CHUNK
    sides = jnp.where(lane < within, near_ref[h : h + 1, 0:1], near_ref[h : h + 1, 510:511])
    row_ref[...] = jnp.broadcast_to(sides, row_ref.shape)
    row_ref[:, pl.ds(pl.multiple_of(within * CHUNK, CHUNK), 3 * CHUNK)] = tiles_ref[h]
    return row_ref[:, CHUNK : CHUNK + MIN_LEN]


def columns_of(dst_ref, base, wq, wk, wv):
    for rows in row_blocks(wq.shape[-1]):
        zero = jnp.zeros((HD, rows.stop - rows.start), BF16)
        dst_ref[base, rows, :] = jnp.transpose(jnp.concatenate([wq[:, rows], zero], 0))
        dst_ref[base + 1, rows, :] = jnp.transpose(
            jnp.concatenate([wk[:, rows], wv[2 * HD : 3 * HD, rows]], 0)
        )
        dst_ref[base + 2, rows, 0 : 2 * HD] = jnp.transpose(wv[0 : 2 * HD, rows])


def front_kernel(
    own,
    xt_ref,
    ogt_ref,
    wq_ref,
    wk_ref,
    wv_ref,
    wo_ref,
    norms_ref,
    mask_ref,
    near_ref,
    q_ref,
    kv_ref,
    mask_out_ref,
    lse_ref,
    pair_ref,
    mid_ref,
    two_ref,
    og_ref,
    lhs_two_ref,
    lhs_og_ref,
    lhs_one_ref,
    square_ref,
    one_ref,
    tall_ref,
    kvt_ref,
    masks_ref,
    tiles_ref,
    row_ref,
    other_o_ref,
    other_wo_ref,
    turned_ref,
    half_ref,
    kv_send,
    kv_recv,
    mask_send,
    mask_recv,
    x_send,
    x_recv,
    core_send,
    core_recv,
):
    ctx = lax.axis_index("ctx")
    wt = lax.axis_index("wt")
    width = xt_ref.shape[0]
    tok = xt_ref.shape[1]
    first_seq = (3 * ctx) // PER
    barrier, count = announce(ctx, wt, (1,))

    def over(src, dst, k):
        return copy_to(src, dst, x_send.at[k], x_recv.at[k], ctx, 1 - wt)

    def core(src, dst, k):
        return copy_to(src, dst, core_send.at[k], core_recv.at[k], flip(ctx, 1), wt)

    def mask_copy(k, peer):
        return copy_to(mask_ref, masks_ref.at[k], mask_send.at[k], mask_recv.at[k], peer, wt)

    def kv_copy(k, i, device, peer):
        g = 3 * device + i
        here = pl.multiple_of((g - PER * ((3 * device) // PER)) * CHUNK, CHUNK)
        there = pl.multiple_of((g - PER * ((3 * peer) // PER)) * CHUNK, CHUNK)
        return copy_to(
            kv_ref.at[pl.ds(here, CHUNK), :],
            kv_ref.at[pl.ds(there, CHUNK), :],
            kv_send.at[k, i],
            kv_recv.at[k, i],
            peer,
            wt,
        )

    def moves(device, i, peer):
        return jnp.logical_and(
            holds(peer, (3 * device + i) // PER), jnp.logical_and(inside(device), inside(peer))
        )

    over_wo = over(wo_ref, other_wo_ref, 0)
    over_o = over(pair_ref.at[0:tok, :], other_o_ref, 1)
    core_og = core(half_ref.at[0], lhs_og_ref.at[:, tok : 2 * tok], 0)
    core_one = core(half_ref.at[1], lhs_one_ref.at[:, tok : 2 * tok], 1)
    core_two = core(half_ref.at[2], lhs_two_ref.at[:, tok : 2 * tok], 2)
    core_o = core(pair_ref.at[0:tok, :], pair_ref.at[tok : 2 * tok, :], 3)

    tall_ref[width:, :] = jnp.zeros((tall_ref.shape[0] - width, tok), F32)
    total = jnp.zeros((1, tok), F32)
    for rows in row_blocks(width):
        x = xt_ref[rows, :].astype(F32)
        total = total + jnp.sum(x * x, axis=0, keepdims=True)
    inverse = lax.rsqrt(total * (1.0 / width) + EPSILON)
    for rows in row_blocks(width):
        h = xt_ref[rows, :].astype(F32) * inverse * gain_of(norms_ref, rows, 0)
        tall_ref[rows, :] = h
        one_ref[rows, :] = h.astype(BF16)
    kt = dot(wk_ref[...], one_ref[...]).astype(BF16)
    vt = dot(wv_ref[...], one_ref[...]).astype(BF16)
    kvt_ref[0 : 3 * HD, :] = kt
    kvt_ref[3 * HD : 4 * HD, :] = vt[2 * HD :, :]
    kvt_ref[4 * HD :, :] = vt[: 2 * HD, :]
    pl.semaphore_wait(barrier, count)
    for k, shift in enumerate(SHIFTS):

        @pl.when(inside(ctx + shift))
        def _():
            mask_copy(k, ctx + shift).start()

    for i in range(3):
        here = pl.multiple_of((3 * ctx + i - PER * first_seq) * CHUNK, CHUNK)
        kv_ref[pl.ds(here, CHUNK), :] = jnp.transpose(kvt_ref[:, i * CHUNK : (i + 1) * CHUNK])
        for k, shift in enumerate(SHIFTS):

            @pl.when(moves(ctx, i, ctx + shift))
            def _():
                kv_copy(k, i, ctx, ctx + shift).start()

    over_wo.start()
    qt = dot(wq_ref[...], one_ref[...]).astype(BF16)
    q_ref[...] = jnp.transpose(jnp.concatenate([qt, jnp.zeros((HD, tok), BF16)], 0))
    arrange(tall_ref, lhs_one_ref, half_ref.at[1], ctx, own)
    core_one.start()
    for rows in row_blocks(width):
        tall_ref[rows, :] = ogt_ref[rows, :].astype(F32)
        og_ref[:, rows] = jnp.transpose(ogt_ref[rows, :])
    arrange(tall_ref, lhs_og_ref, half_ref.at[0], ctx, own)
    core_og.start()
    for rows in row_blocks(width):
        count = rows.stop - rows.start
        turned_ref[0, rows, :] = jnp.transpose(
            jnp.concatenate([wo_ref[:, rows], jnp.zeros((HD, count), BF16)], 0)
        )
    near_tiles(near_ref, tiles_ref)
    masks_ref[len(SHIFTS)] = mask_ref[...]

    @pl.when((3 * ctx + 2) // PER == first_seq)
    def _():
        kv_ref[MIN_LEN:, :] = jnp.zeros((MIN_LEN, 6 * HD), BF16)

    for k, shift in enumerate(SHIFTS):
        source = ctx - shift

        @pl.when(inside(source))
        def _():
            mask_copy(k, source).wait_recv()

        for i in range(3):

            @pl.when(moves(source, i, ctx))
            def _():
                g = 3 * source + i
                there = pl.multiple_of((g - PER * first_seq) * CHUNK, CHUNK)
                spot = kv_ref.at[pl.ds(there, CHUNK), :]
                copy_to(spot, spot, kv_send.at[k, i], kv_recv.at[k, i], source, wt).wait_recv()

    for c in range(2 * PER):
        g = PER * first_seq + c
        row = jnp.zeros((1, CHUNK), F32)
        for k, shift in enumerate((*SHIFTS, 0)):
            for i in range(3):
                match = jnp.logical_and(g // 3 == ctx - shift, g % 3 == i)
                row = jnp.where(match, masks_ref[k, 0:1, i * CHUNK : (i + 1) * CHUNK], row)
        mask_out_ref[0:1, c * CHUNK : (c + 1) * CHUNK] = row
    for i in range(3):
        rows = slice(i * CHUNK, (i + 1) * CHUNK)
        g = 3 * ctx + i
        window = pl.multiple_of((g // PER - first_seq) * MIN_LEN, MIN_LEN)
        q = q_ref[rows, :]
        keys = kv_ref[pl.ds(window, MIN_LEN), 0:256]
        values = kv_ref[pl.ds(window, MIN_LEN), 128:384]
        mask = mask_out_ref[:, pl.ds(window, MIN_LEN)]
        out = jnp.zeros((CHUNK, 256), F32)
        lse = jnp.zeros((CHUNK, CHUNK), F32)
        for h in range(3):
            s = mat_t(jnp.where(head_lanes(q.shape, h, False), q, jnp.zeros_like(q)), keys)
            s = s + bias_row(near_ref, tiles_ref, row_ref, h, g % PER) + mask
            top = jnp.max(s, axis=1, keepdims=True)
            e = jnp.exp(s - top)
            sums = jnp.sum(e, axis=1, keepdims=True)
            p = (e * (1.0 / sums)).astype(BF16)
            out = jnp.where(head_lanes(out.shape, h, True), dot(p, values), out)
            lse = jnp.where(iota(lse.shape, 1) == h, top + jnp.log(sums), lse)
        late = pltpu.roll(out[:, 0:128], HD, 1)
        late = jnp.where(iota(late.shape, 1) < HD, late, 0.0)
        pair_ref[rows, 0:128] = out[:, 128:256].astype(BF16)
        pair_ref[rows, 128:256] = late.astype(BF16)
        lse_ref[rows, :] = lse
    over_o.start()
    core_o.start()
    over_wo.wait_recv()
    for rows in row_blocks(width):
        count = rows.stop - rows.start
        turned_ref[1, rows, :] = jnp.transpose(
            jnp.concatenate([other_wo_ref[:, rows], jnp.zeros((HD, count), BF16)], 0)
        )
    over_o.wait_recv()
    total = jnp.zeros((1, tok), F32)
    squares = jnp.zeros((1, tok), F32)
    for rows in row_blocks(width, 368):
        branch = mat_t(turned_ref[0, rows, :], pair_ref[0:tok, :]) + mat_t(
            turned_ref[1, rows, :], other_o_ref[...]
        )
        mid = xt_ref[rows, :].astype(F32) + branch
        mid_ref[rows, :] = mid
        total = total + jnp.sum(mid * mid, axis=0, keepdims=True)
        squares = squares + jnp.sum(branch * branch, axis=0, keepdims=True)
    square_ref[...] = jnp.broadcast_to(jnp.sum(squares, axis=1, keepdims=True), square_ref.shape)
    inverse = lax.rsqrt(total * (1.0 / width) + EPSILON)
    for rows in row_blocks(width):
        h = mid_ref[rows, :] * inverse * gain_of(norms_ref, rows, 1)
        tall_ref[rows, :] = h
        two_ref[:, rows] = jnp.transpose(h.astype(BF16))
    arrange(tall_ref, lhs_two_ref, half_ref.at[2], ctx, own)
    core_two.start()
    for each in (core_og, core_one, core_o, core_two):
        each.wait()
    for each in (over_wo, over_o):
        each.wait_send()
    for k, shift in enumerate(SHIFTS):

        @pl.when(inside(ctx + shift))
        def _():
            mask_copy(k, ctx + shift).wait_send()

        for i in range(3):

            @pl.when(moves(ctx, i, ctx + shift))
            def _():
                kv_copy(k, i, ctx, ctx + shift).wait_send()


def in_vmem():
    return pl.BlockSpec(memory_space=pltpu.VMEM)


def anywhere():
    return pl.BlockSpec(memory_space=pl.ANY)


def shape_of(shape, dtype):
    return jax.ShapeDtypeStruct(shape, dtype)


def front(xt, ogt, wq, wk, wv, wo, norms, mask, near):
    width, tok = xt.shape
    own = width // 16
    rows = 8 * (-(-own // 16) * 16)
    out_shape = (
        shape_of((tok, 256), BF16),
        shape_of((2 * MIN_LEN, 384), BF16),
        shape_of((1, 2 * MIN_LEN), F32),
        shape_of((tok, CHUNK), F32),
        shape_of((2 * tok, 256), BF16),
        shape_of((width, tok), F32),
        shape_of((tok, width), BF16),
        shape_of((tok, width), BF16),
        shape_of((rows, 2 * tok), BF16),
        shape_of((rows, 2 * tok), BF16),
        shape_of((rows, 2 * tok), BF16),
        shape_of((8, CHUNK), F32),
    )
    dma = pltpu.SemaphoreType.DMA
    return pl.pallas_call(
        partial(front_kernel, own),
        out_shape=out_shape,
        in_specs=[in_vmem()] * 9,
        out_specs=(in_vmem(),) * len(out_shape),
        scratch_shapes=[
            pltpu.VMEM((width, tok), BF16),
            pltpu.VMEM((width + 16, tok), F32),
            pltpu.VMEM((384, tok), BF16),
            pltpu.VMEM((len(SHIFTS) + 1, 8, tok), F32),
            pltpu.VMEM((3, CHUNK, 3 * CHUNK), F32),
            pltpu.VMEM((CHUNK, MIN_LEN + 2 * CHUNK), F32),
            pltpu.VMEM((tok, 256), BF16),
            pltpu.VMEM((192, width), BF16),
            pltpu.VMEM((2, width, 256), BF16),
            pltpu.VMEM((3, rows, tok), BF16),
            dma((len(SHIFTS), 3)),
            dma((len(SHIFTS), 3)),
            dma((len(SHIFTS),)),
            dma((len(SHIFTS),)),
            dma((2,)),
            dma((2,)),
            dma((4,)),
            dma((4,)),
        ],
        compiler_params=pltpu.CompilerParams(
            collective_id=1, has_side_effects=True, vmem_limit_bytes=56 << 20
        ),
        cost_estimate=pl.CostEstimate(
            flops=8 * tok * width * 640, bytes_accessed=20 << 20, transcendentals=3 << 20
        ),
        name="front",
    )(xt, ogt, wq, wk, wv, wo, norms, mask, near)


GROUPS = 7
TILES = 24
SMALL = 104
NEAR_ROW, FAR_ROW, SQUARE_ROW, ONE_ROW, TWO_ROW = 56, 68, 74, 80, 92
RING = 6
AHEAD = 3


def back_kernel(
    own,
    two_ref,
    og_ref,
    mid_ref,
    norms_ref,
    q_ref,
    lse_ref,
    pair_ref,
    wo_ref,
    wq_ref,
    wk_ref,
    wv_ref,
    mask_ref,
    near_ref,
    square_ref,
    gate_hbm,
    up_hbm,
    down_hbm,
    lhs_two_hbm,
    lhs_og_hbm,
    lhs_one_hbm,
    kv_hbm,
    ogt_hbm,
    xt_hbm,
    down_out,
    gate_out,
    up_out,
    tail_out,
    y_out,
    dx_out,
    small_ref,
    lhs_two_ref,
    lhs_og_ref,
    keep_ref,
    rhs_ref,
    first_ref,
    second_ref,
    third_ref,
    stream_ref,
    grad_ref,
    acc_ref,
    over_ref,
    got_ref,
    side_ref,
    kv_ref,
    back_ref,
    tiles_ref,
    pad_ref,
    diag_ref,
    dqkv_ref,
    lhs_da_ref,
    half_ref,
    other_w_ref,
    small_got_ref,
    step_send,
    step_recv,
    rhs_send,
    rhs_recv,
    free_sem,
    load_sem,
    local_sem,
    x_send,
    x_recv,
    back_send,
    back_recv,
    core_send,
    core_recv,
    small_send,
    small_recv,
):
    ctx = lax.axis_index("ctx")
    wt = lax.axis_index("wt")
    width, tok = mid_ref.shape
    first_seq = (3 * ctx) // PER
    blocks = row_blocks(width)
    barrier, count = announce(ctx, wt, (1, 2, 4, 8))

    def over(src, dst, k):
        return copy_to(src, dst, x_send.at[k], x_recv.at[k], ctx, 1 - wt)

    def core(src, dst, k):
        return copy_to(src, dst, core_send.at[k], core_recv.at[k], flip(ctx, 1), wt)

    over_w = [over(w, other_w_ref.at[k], k) for k, w in enumerate((wq_ref, wk_ref, wv_ref))]
    over_two = over(over_ref.at[0], got_ref.at[0], 3)
    over_f = over(over_ref.at[1], got_ref.at[1], 4)
    over_dqkv = over(dqkv_ref.at[0], dqkv_ref.at[1], 5)
    core_da = core(half_ref, lhs_da_ref.at[:, tok : 2 * tok], 0)
    load_kv = pltpu.make_async_copy(kv_hbm, kv_ref, local_sem.at[0])
    load_og = pltpu.make_async_copy(ogt_hbm, side_ref, local_sem.at[1])
    load_x = pltpu.make_async_copy(xt_hbm, side_ref, local_sem.at[2])
    load_left = (
        pltpu.make_async_copy(lhs_two_hbm, lhs_two_ref, local_sem.at[3]),
        pltpu.make_async_copy(lhs_og_hbm, lhs_og_ref, local_sem.at[4]),
    )
    load_one = pltpu.make_async_copy(lhs_one_hbm, lhs_og_ref, local_sem.at[5])
    save_y = pltpu.make_async_copy(got_ref.at[1], y_out, local_sem.at[6])
    save_dx = pltpu.make_async_copy(got_ref.at[0], dx_out, local_sem.at[7])

    def load(j, m):
        slot = j % 2
        source = (gate_hbm, up_hbm, down_hbm)[m]
        return pltpu.make_async_copy(
            source.at[:, pl.ds(multiple(j * TILE, TILE), TILE)],
            stream_ref.at[slot * 3 + m],
            load_sem.at[slot, m],
        )

    def step_copy(s, t):
        late = (t % 6) // 5
        bit = (2 + 2 * late, 4 + 4 * late, 8 - 6 * late)[s]
        low, high = ((384, 768), (192, 384), (96, 192))[s]
        return copy_to(
            keep_ref.at[t, low:high, :],
            (first_ref, second_ref, third_ref)[s].at[t],
            step_send.at[s, t],
            step_recv.at[s, t],
            flip(ctx, bit),
            wt,
        )

    def add_in(s, t):
        rows = (384, 192)[s]
        got = (first_ref, second_ref)[s]
        step_copy(s, t).wait_recv()
        total = keep_ref[t, 0:rows, :].astype(F32) + got[t].astype(F32)
        keep_ref[t, 0:rows, :] = total.astype(BF16)

    def finish(t):
        step_copy(2, t).wait_recv()
        total = keep_ref[t, 0:96, :].astype(F32) + third_ref[t].astype(F32)
        if isinstance(t, int) and t >= 3 * GROUPS:
            tail_out[:, (t - 3 * GROUPS) * TILE : (t - 3 * GROUPS + 1) * TILE] = total
            return
        lanes = pl.ds(multiple((t // 3) * TILE, TILE), TILE)
        for m, out in enumerate((down_out, gate_out, up_out)):

            def write(out=out):
                out[:, lanes] = total[0:own]

            if isinstance(t, int):
                if t % 3 == m:
                    write()
            else:
                pl.when(t % 3 == m)(write)

    def step(k):
        if k + AHEAD < TILES:
            step_copy(0, k + AHEAD).start()
        if k < TILES:
            add_in(0, k)
            step_copy(1, k).start()
        if 1 <= k <= TILES:
            add_in(1, k - 1)
            step_copy(2, k - 1).start()
        if k >= 2:
            finish(k - 2)

    def rhs_copy(slot):
        return copy_to(
            rhs_ref.at[slot, 0:tok, :],
            rhs_ref.at[slot, tok : 2 * tok, :],
            rhs_send.at[slot],
            rhs_recv.at[slot],
            flip(ctx, 1),
            wt,
        )

    def put_tile(t, result, late):
        if not late:
            keep_ref[t] = result
            return
        for b in range(8):
            place = (b % 4) * 2 + b // 4
            keep_ref[t, place * 96 : (place + 1) * 96, :] = result[b * 96 : (b + 1) * 96]

    def credit():
        pl.semaphore_signal(free_sem, inc=1, device_id=(flip(ctx, 1), wt), device_id_type=MESH)

    def products(j):
        for m in range(3):
            slot = (j % 2) * 3 + m
            rhs_copy(slot).wait_recv()
            lhs = lhs_og_ref if m == 0 else lhs_two_ref
            result = dot(lhs[...], rhs_ref[slot]).astype(BF16)
            if m < 2:
                put_tile(3 * j + m, result, False)
            elif isinstance(j, int):
                put_tile(3 * j + m, result, j % 2 == 1)
            else:
                pl.when(j % 2 == 1)(lambda: put_tile(3 * j + 2, result, True))
                pl.when(j % 2 == 0)(lambda: put_tile(3 * j + 2, result, False))

    def reuse_slots(j):
        for m in range(3):
            rhs_copy((j % 2) * 3 + m).wait_send()
        pl.semaphore_wait(free_sem, 1)

    for m in range(3):
        load(0, m).start()
    for each in load_left:
        each.start()
    load_kv.start()
    load_og.start()
    grad_ref[...] = jnp.zeros_like(grad_ref)
    acc_ref[...] = jnp.zeros_like(acc_ref)
    pl.semaphore_wait(barrier, count)
    for each in over_w:
        each.start()

    def group(j, carry):
        slot = (j % 2) * 3
        for m in range(3):
            load(j, m).wait()

        @pl.when(j < GROUPS - 1)
        def _():
            for m in range(3):
                load(j + 1, m).start()

        @pl.when(j >= 2)
        def _():
            reuse_slots(j)

        gate = dot(two_ref[...], stream_ref[slot])
        up = dot(two_ref[...], stream_ref[slot + 1])
        dhid = dot(og_ref[...], stream_ref[slot + 2])
        square = gate * gate
        bend = jnp.tanh(GELU * gate * (1.0 + CUBIC * square))
        half = 0.5 * (1.0 + bend)
        unit = gate * half
        slope = half + (0.5 * GELU) * gate * (1.0 - bend * bend) * (1.0 + 3.0 * CUBIC * square)
        rhs_ref[slot, 0:tok, :] = (unit * up).astype(BF16)
        rhs_ref[slot + 1, 0:tok, :] = (dhid * up * slope).astype(BF16)
        rhs_ref[slot + 2, 0:tok, :] = (dhid * unit).astype(BF16)
        for m in range(3):
            rhs_copy(slot + m).start()
        for rows in row_blocks(width, 368):
            grad_ref[rows, :] += mat_t(stream_ref[slot + 1, rows, :], rhs_ref[slot + 2, 0:tok, :]) + mat_t(
                stream_ref[slot, rows, :], rhs_ref[slot + 1, 0:tok, :]
            )
            acc_ref[rows, :] += mat_t(stream_ref[slot + 2, rows, :], rhs_ref[slot, 0:tok, :])

        @pl.when(j == 1)
        def _():
            for each in load_left:
                each.wait()

        @pl.when(j >= 1)
        def _():
            products(j - 1)
            credit()

        @pl.when(j == 1)
        def _():
            for t in range(AHEAD):
                step_copy(0, t).start()

        @pl.when(j >= 2)
        def _():
            k = j - 2
            step_copy(0, k + AHEAD).start()
            add_in(0, k)
            step_copy(1, k).start()

            @pl.when(j >= 3)
            def _():
                add_in(1, k - 1)
                step_copy(2, k - 1).start()

            @pl.when(j >= 4)
            def _():
                finish(k - 2)

        return carry

    lax.fori_loop(0, GROUPS, group, 0)
    for rows in blocks:
        over_ref[0, rows, :] = grad_ref[rows, :].astype(BF16)
    for each in over_w:
        each.wait_recv()
    over_two.start()
    for rows in blocks:
        over_ref[1, rows, :] = acc_ref[rows, :].astype(BF16)
    products(GROUPS - 1)
    load_one.start()
    columns_of(stream_ref, 0, wq_ref, wk_ref, wv_ref)
    columns_of(stream_ref, 3, other_w_ref.at[0], other_w_ref.at[1], other_w_ref.at[2])
    acc_ref[...] = jnp.zeros_like(acc_ref)
    small_ref[...] = jnp.zeros_like(small_ref)
    diag_ref[...] = jnp.zeros_like(diag_ref)
    near_tiles(near_ref, tiles_ref)
    total = jnp.zeros((1, tok), F32)
    for rows in blocks:
        total = total + jnp.sum(mid_ref[rows, :] * mid_ref[rows, :], axis=0, keepdims=True)
    inverse = lax.rsqrt(total * (1.0 / width) + EPSILON)
    for k in range(5, 10):
        step(k)

    def lane_sums(x, row, rows):
        folded = x[:, 0:128] + x[:, 128:256] + x[:, 256:384]
        place = rows.start // CHUNK
        count = rows.stop - rows.start
        small_ref[row + place : row + place + 1, 0:count] = jnp.sum(
            jnp.transpose(folded), axis=0, keepdims=True
        )

    over_two.wait()
    over_f.start()
    mean = jnp.zeros((1, tok), F32)
    for rows in blocks:
        d = over_ref[0, rows, :].astype(F32) + got_ref[0, rows, :].astype(F32)
        normed = mid_ref[rows, :] * inverse
        lane_sums(d * normed, TWO_ROW, rows)
        d = d * gain_of(norms_ref, rows, 1)
        grad_ref[rows, :] = d
        mean = mean + jnp.sum(d * normed, axis=0, keepdims=True)
    mean = mean * (1.0 / width)
    load_og.wait()
    for rows in blocks:
        normed = mid_ref[rows, :] * inverse
        d = side_ref[rows, :].astype(F32) + inverse * (grad_ref[rows, :] - normed * mean)
        grad_ref[rows, :] = d
        over_ref[0, rows, :] = d.astype(BF16)
    load_x.start()
    dotted = dot(wo_ref[...], over_ref[0]).astype(BF16)
    turned = jnp.transpose(
        jnp.concatenate([jnp.zeros((HD, tok), BF16), dotted[2 * HD :], dotted[: 2 * HD]], 0)
    )
    dqkv_ref[0, :, 0:256] = turned
    arrange(grad_ref, lhs_da_ref, half_ref, ctx, own)
    core_da.start()
    load_kv.wait()
    step(10)

    far = [jnp.zeros((1, MIN_LEN), F32) for _ in range(6)]
    for i in range(3):
        rows = slice(i * CHUNK, (i + 1) * CHUNK)
        g = 3 * ctx + i
        within = g % PER
        window = pl.multiple_of((g // PER - first_seq) * MIN_LEN, MIN_LEN)
        q = q_ref[rows, :]
        do = dqkv_ref[0, rows, 0:256]
        keys = kv_ref[pl.ds(window, MIN_LEN), 0:256]
        values = kv_ref[pl.ds(window, MIN_LEN), 128:384]
        mask = mask_ref[:, pl.ds(window, MIN_LEN)]
        column = iota((1, MIN_LEN), 1) // CHUNK
        dq = jnp.zeros((CHUNK, 256), F32)
        dmask = jnp.zeros((1, MIN_LEN), F32)
        for h in range(3):
            qm = jnp.where(head_lanes(q.shape, h, False), q, jnp.zeros_like(q))
            dom = jnp.where(head_lanes(do.shape, h, True), do, jnp.zeros_like(do))
            s = mat_t(qm, keys) + bias_row(near_ref, tiles_ref, pad_ref, h, within) + mask
            p = jnp.exp(s - lse_ref[rows, h : h + 1])
            dp = mat_t(dom, values)
            delta = jnp.sum(p * dp, axis=1, keepdims=True)
            ds = p * (dp - delta)
            low = ds.astype(BF16)
            dq = jnp.where(head_lanes(dq.shape, h, False), dot(low, keys), dq)
            acc_ref[pl.ds(window, MIN_LEN), 0:256] += t_mat(low, qm)
            acc_ref[pl.ds(window, MIN_LEN), 128:384] += t_mat(p.astype(BF16), dom)
            sums = jnp.sum(ds, axis=0, keepdims=True)
            dmask = dmask + sums
            far[2 * h] = far[2 * h] + jnp.where(column < within - 1, sums, 0.0)
            far[2 * h + 1] = far[2 * h + 1] + jnp.where(column > within + 1, sums, 0.0)
            pad_ref[:, 0:CHUNK] = jnp.zeros((CHUNK, CHUNK), F32)
            pad_ref[:, CHUNK : CHUNK + MIN_LEN] = ds
            pad_ref[:, MIN_LEN + CHUNK :] = jnp.zeros((CHUNK, CHUNK), F32)
            near = pl.multiple_of(within * CHUNK, CHUNK)
            diag_ref[h, :, 0 : 3 * CHUNK] += pad_ref[:, pl.ds(near, 3 * CHUNK)]
        dqkv_ref[0, rows, 0:256] = dq.astype(BF16)
        spots = pl.ds(pl.multiple_of((g // PER) * PER, PER), PER)
        small_ref[spots, :] += jnp.concatenate(
            [dmask[:, c * CHUNK : (c + 1) * CHUNK] for c in range(PER)], 0
        )
        step(11 + i)

    def back_copy(k, i, sender, owner):
        g = 3 * owner + i
        spot = pl.multiple_of((g - PER * ((3 * sender) // PER)) * CHUNK, CHUNK)
        return copy_to(
            kv_ref.at[pl.ds(spot, CHUNK), :],
            back_ref.at[k, i],
            back_send.at[k, i],
            back_recv.at[k, i],
            owner,
            wt,
        )

    def moves(sender, i, owner):
        return jnp.logical_and(
            holds(sender, (3 * owner + i) // PER),
            jnp.logical_and(inside(sender), inside(owner)),
        )

    kv_ref[...] = acc_ref[...].astype(BF16)
    for k, shift in enumerate(SHIFTS):
        for i in range(3):

            @pl.when(moves(ctx, i, ctx + shift))
            def _():
                back_copy(k, i, ctx, ctx + shift).start()

    for h in range(3):
        tile = diag_ref[h]
        count = CHUNK
        while count > 1:
            count //= 2
            tile = tile[:count] + pltpu.roll(tile[count:], 512 - count, 1)
        for c in range(4):
            row = NEAR_ROW + 4 * h + c
            small_ref[row : row + 1, :] = tile[:, c * CHUNK : (c + 1) * CHUNK]
        for side in range(2):
            row = FAR_ROW + 2 * h + side
            small_ref[row : row + 1, :] = jnp.broadcast_to(
                jnp.sum(far[2 * h + side], axis=1, keepdims=True), (1, CHUNK)
            )
    step(14)
    first = pl.multiple_of((3 * ctx - PER * first_seq) * CHUNK, CHUNK)
    for k, shift in enumerate(SHIFTS):
        for i in range(3):

            @pl.when(moves(ctx - shift, i, ctx))
            def _():
                spot = kv_ref.at[pl.ds(first, CHUNK), :]
                copy_to(
                    spot, back_ref.at[k, i], back_send.at[k, i], back_recv.at[k, i], ctx - shift, wt
                ).wait_recv()
                place = pl.multiple_of(first + i * CHUNK, CHUNK)
                acc_ref[pl.ds(place, CHUNK), :] += back_ref[k, i].astype(F32)

    dqkv_ref[0, :, 256:640] = acc_ref[pl.ds(first, tok), :].astype(BF16)
    over_dqkv.start()

    reuse_slots(GROUPS)
    rhs_ref[3, 0:tok, :] = dqkv_ref[0, :, 0:256]
    rhs_ref[4, 0:tok, :] = dqkv_ref[0, :, 256:512]
    rhs_ref[5, 0:tok, 0:128] = dqkv_ref[0, :, 512:640]
    rhs_ref[5, 0:tok, 128:256] = jnp.zeros((tok, 128), BF16)
    for m in range(3):
        rhs_copy(3 + m).start()
    step(15)
    core_da.wait()
    load_one.wait()
    zero = jnp.zeros((2 * tok, 128), BF16)
    late = pltpu.roll(pair_ref[:, 128:256].astype(F32), HD, 1).astype(BF16)
    extra = (jnp.concatenate([zero, late], 1), None, jnp.concatenate([zero, pair_ref[:, 0:128]], 1))
    for m in range(3):
        rhs_copy(3 + m).wait_recv()
        result = dot(lhs_og_ref[...], rhs_ref[3 + m])
        if extra[m] is not None:
            result = result + dot(lhs_da_ref[...], extra[m])
        put_tile(3 * GROUPS + m, result.astype(BF16), m == 2)
    for k in range(16, 19):
        step(k)

    over_dqkv.wait_recv()
    load_x.wait()
    total = jnp.zeros((1, tok), F32)
    for rows in blocks:
        x = side_ref[rows, :].astype(F32)
        total = total + jnp.sum(x * x, axis=0, keepdims=True)
    inverse = lax.rsqrt(total * (1.0 / width) + EPSILON)
    mean = jnp.zeros((1, tok), F32)
    for part in row_blocks(width, 368):
        sides = []
        for turn in range(2):
            side = (wt + turn) % 2
            sides.append(
                mat_t(stream_ref[3 * side, part, :], dqkv_ref[side, :, 0:256])
                + mat_t(stream_ref[3 * side + 1, part, :], dqkv_ref[side, :, 256:512])
                + mat_t(stream_ref[3 * side + 2, part, 0:128], dqkv_ref[side, :, 512:640])
            )
        acc_ref[part, :] = sides[0] + sides[1]
    for rows in blocks:
        d = acc_ref[rows, :]
        normed = side_ref[rows, :].astype(F32) * inverse
        lane_sums(d * normed, ONE_ROW, rows)
        d = d * gain_of(norms_ref, rows, 0)
        acc_ref[rows, :] = d
        mean = mean + jnp.sum(d * normed, axis=0, keepdims=True)
    mean = mean * (1.0 / width)
    for rows in blocks:
        normed = side_ref[rows, :].astype(F32) * inverse
        d = grad_ref[rows, :] + inverse * (acc_ref[rows, :] - normed * mean)
        got_ref[0, rows, :] = d.astype(BF16)
    save_dx.start()
    step(19)

    over_f.wait()
    y_sum = jnp.zeros((1, tok), F32)
    f_sum = jnp.zeros((1, tok), F32)
    for rows in blocks:
        f = over_ref[1, rows, :].astype(F32) + got_ref[1, rows, :].astype(F32)
        y = mid_ref[rows, :] + f
        got_ref[1, rows, :] = y.astype(BF16)
        y_sum = y_sum + jnp.sum(y * y, axis=0, keepdims=True)
        f_sum = f_sum + jnp.sum(f * f, axis=0, keepdims=True)
    save_y.start()
    for k, sums in enumerate((y_sum, f_sum)):
        row = SQUARE_ROW + 2 * k
        small_ref[row : row + 1, :] = jnp.broadcast_to(
            jnp.sum(sums, axis=1, keepdims=True), (1, CHUNK)
        )
    small_ref[SQUARE_ROW + 1 : SQUARE_ROW + 2, :] = square_ref[0:1, :]

    for r in range(5):
        rows = SMALL if r < 4 else NEAR_ROW
        peer = (flip(ctx, 1 << r), wt) if r < 4 else (ctx, 1 - wt)
        both = copy_to(
            small_ref.at[0:rows, :],
            small_got_ref.at[r, 0:rows, :],
            small_send.at[r],
            small_recv.at[r],
            *peer,
        )
        both.start()
        step(20 + r)
        both.wait()
        small_ref[0:rows, :] = small_ref[0:rows, :] + small_got_ref[r, 0:rows, :]
    step(25)

    for t in range(TILES):
        for s in range(3):
            step_copy(s, t).wait_send()
    for slot in range(RING):
        rhs_copy(slot).wait_send()
    save_y.wait()
    save_dx.wait()
    over_dqkv.wait_send()
    for each in over_w:
        each.wait_send()
    for k, shift in enumerate(SHIFTS):
        for i in range(3):

            @pl.when(moves(ctx, i, ctx + shift))
            def _():
                back_copy(k, i, ctx, ctx + shift).wait_send()


def back(inputs_here, own):
    width, tok = inputs_here[2].shape
    rows = 8 * (-(-own // 16) * 16)
    hidden = inputs_here[14].shape[1]
    out_shape = (
        shape_of((own, hidden), F32),
        shape_of((own, hidden), F32),
        shape_of((own, hidden), F32),
        shape_of((rows // 8, 3 * TILE), F32),
        shape_of((width, tok), BF16),
        shape_of((width, tok), BF16),
        shape_of((SMALL, CHUNK), F32),
    )
    dma = pltpu.SemaphoreType.DMA
    return pl.pallas_call(
        partial(back_kernel, own),
        out_shape=out_shape,
        in_specs=[in_vmem()] * 14 + [anywhere()] * 9,
        out_specs=(in_vmem(),) * 4 + (anywhere(),) * 2 + (in_vmem(),),
        scratch_shapes=[
            pltpu.VMEM((rows, 2 * tok), BF16),
            pltpu.VMEM((rows, 2 * tok), BF16),
            pltpu.VMEM((TILES, rows, TILE), BF16),
            pltpu.VMEM((RING, 2 * tok, TILE), BF16),
            pltpu.VMEM((TILES, rows // 2, TILE), BF16),
            pltpu.VMEM((TILES, rows // 4, TILE), BF16),
            pltpu.VMEM((TILES, rows // 8, TILE), BF16),
            pltpu.VMEM((6, width, TILE), BF16),
            pltpu.VMEM((width + 16, tok), F32),
            pltpu.VMEM((2 * MIN_LEN, tok), F32),
            pltpu.VMEM((2, width, tok), BF16),
            pltpu.VMEM((2, width, tok), BF16),
            pltpu.VMEM((width, tok), BF16),
            pltpu.VMEM((2 * MIN_LEN, 384), BF16),
            pltpu.VMEM((len(SHIFTS), 3, CHUNK, 384), BF16),
            pltpu.VMEM((3, CHUNK, 3 * CHUNK), F32),
            pltpu.VMEM((CHUNK, MIN_LEN + 2 * CHUNK), F32),
            pltpu.VMEM((3, CHUNK, 512), F32),
            pltpu.VMEM((2, tok, 640), BF16),
            pltpu.VMEM((rows, 2 * tok), BF16),
            pltpu.VMEM((rows, tok), BF16),
            pltpu.VMEM((3, 192, width), BF16),
            pltpu.VMEM((5, SMALL, CHUNK), F32),
            dma((3, TILES)),
            dma((3, TILES)),
            dma((RING,)),
            dma((RING,)),
            pltpu.SemaphoreType.REGULAR,
            dma((2, 3)),
            dma((8,)),
            dma((6,)),
            dma((6,)),
            dma((len(SHIFTS), 3)),
            dma((len(SHIFTS), 3)),
            dma((1,)),
            dma((1,)),
            dma((5,)),
            dma((5,)),
        ],
        compiler_params=pltpu.CompilerParams(
            collective_id=2, has_side_effects=True, vmem_limit_bytes=64 << 20
        ),
        cost_estimate=pl.CostEstimate(
            flops=20 * 10**9, bytes_accessed=40 << 20, transcendentals=8 << 20
        ),
        name="back",
    )(*inputs_here)


def even(
    inputs,
    delete_mask,
    lengths,
    dealing,
    w_query,
    w_key,
    w_value,
    w_output,
    bias_table,
    norm_attn,
    w_gate,
    w_up,
    w_down,
    norm_ffn,
    out_grad,
):
    tok, width = inputs.shape
    n = lax.axis_size("ctx")
    ctx = lax.axis_index("ctx")
    own = width // n
    tokens_all = tok * n
    ids = jnp.arange(bias_table.shape[0], dtype=jnp.int32)

    def chosen(offsets):
        return bucket_of(offsets)[:, None] == ids[None, :]

    places_near = chosen(jnp.arange(512, dtype=jnp.int32) - 255)
    near = jnp.sum(jnp.where(places_near[None], jnp.transpose(bias_table)[:, None, :], 0.0), -1)
    near = jnp.pad(near, ((0, 5), (0, 0)))
    mask = jnp.broadcast_to(delete_mask.astype(F32)[None], (8, tok))
    norms = jnp.pad(jnp.stack([norm_attn, norm_ffn]), ((0, 6), (0, 0)))
    xt = jnp.transpose(inputs)
    ogt = jnp.transpose(out_grad)
    wq = jnp.transpose(w_query)
    wk = jnp.transpose(w_key)
    wv = jnp.transpose(w_value)
    q, kv, masks, lse, pair, mid, two, og, lhs_two, lhs_og, lhs_one, square = front(
        xt, ogt, wq, wk, wv, w_output, norms, mask, near
    )
    down, gate, up, tail, y, dx, small = back(
        (
            two,
            og,
            mid,
            norms,
            q,
            lse,
            pair,
            w_output,
            wq,
            wk,
            wv,
            masks,
            near,
            square,
            w_gate,
            w_up,
            jnp.transpose(w_down),
            lhs_two,
            lhs_og,
            lhs_one,
            kv,
            ogt,
            xt,
        ),
        own,
    )
    mask_all = small[: tokens_all // CHUNK].reshape(n, 1, tok)
    quota = tok // n
    slots = lax.dynamic_slice_in_dim(dealing, ctx * tok, tok).reshape(n, quota, 1)
    slots = slots - (jnp.arange(n, dtype=jnp.int32) * tok)[:, None, None]
    picked = slots == jnp.arange(tok, dtype=jnp.int32)[None, None, :]
    mask_grad = jnp.sum(jnp.where(picked, mask_all, 0.0), axis=-1).reshape(tok)
    offsets = jnp.arange(512, dtype=jnp.int32)
    offsets = jnp.where(offsets < 3 * CHUNK, offsets, offsets - 512) - CHUNK
    diagonals = small[NEAR_ROW:FAR_ROW].reshape(3, 512)
    table = jnp.sum(jnp.where(chosen(offsets)[None], diagonals[:, :, None], 0.0), axis=1)
    far = small[FAR_ROW : FAR_ROW + 6, 0].reshape(3, 2)
    table = table + jnp.where(ids == 15, 1.0, 0.0)[None] * far[:, :1]
    table = table + jnp.where(ids == 31, 1.0, 0.0)[None] * far[:, 1:]
    gains = small[ONE_ROW : ONE_ROW + 24].reshape(2, 12 * CHUNK)
    gains = lax.dynamic_slice_in_dim(gains, ctx * own, own, axis=1)
    root_means = jnp.sqrt(small[SQUARE_ROW : SQUARE_ROW + 3, 0] / (tokens_all * width))
    tail = tail[:own]
    return (
        jnp.transpose(y),
        jnp.transpose(dx),
        mask_grad.astype(BF16),
        tail[:, :192],
        tail[:, 256:448],
        jnp.concatenate([tail[:, 512:640], tail[:, 448:512]], axis=1),
        jnp.transpose(jnp.concatenate([tail[:, 640:768], tail[:, 192:256]], axis=1)),
        jnp.transpose(table),
        gains[0],
        gate,
        up,
        jnp.transpose(down),
        gains[1],
        root_means,
    )


def local(inputs, delete_mask, lengths, *rest):
    tok = inputs.shape[0]
    fits = lax.axis_size("ctx") == 16 and lax.axis_size("wt") == 2 and tok == 3 * CHUNK
    fits = fits and tok * 16 == MIN_LEN * lengths.shape[0] and inputs.shape[1] == 1472
    fits = fits and rest[1].shape[1] == 3 * HD and rest[7].shape[1] == GROUPS * TILE
    return (even if fits else general)(inputs, delete_mask, lengths, *rest)


def solution(mesh):
    return jax.shard_map(
        local,
        mesh=mesh,
        in_specs=(
            P("ctx", None),
            P("ctx"),
            P(),
            P(),
            P(None, "wt"),
            P(None, "wt"),
            P(None, "wt"),
            P("wt", None),
            P(None, "wt"),
            P(),
            P(None, "wt"),
            P(None, "wt"),
            P("wt", None),
            P(),
            P("ctx", None),
        ),
        out_specs=(
            P("ctx", None),
            P("ctx", None),
            P("ctx"),
            P("ctx", "wt"),
            P("ctx", "wt"),
            P("ctx", "wt"),
            P("wt", "ctx"),
            P(None, "wt"),
            P("ctx"),
            P("ctx", "wt"),
            P("ctx", "wt"),
            P("wt", "ctx"),
            P("ctx"),
            P(),
        ),
        check_vma=False,
    )
```

```python
from functools import partial

import jax
import jax.numpy as jnp
from jax import lax
from jax.experimental import pallas as pl
from jax.experimental.pallas import tpu as pltpu
from jax.sharding import PartitionSpec as P

HD = 64
MIN_LEN = 1024
CHUNK = 128
THRESHOLDS = (1, 2, 3, 4, 5, 6, 7, 8, 12, 16, 23, 32, 46, 64, 91)
MASKED = -1e30
EPSILON = 1e-06
F32 = jnp.float32
BF16 = jnp.bfloat16


def bucket_of(offset):
    distance = jnp.abs(offset)
    bucket_sum = (offset > 0).astype(jnp.int32) * 16
    for threshold in THRESHOLDS:
        bucket_sum = bucket_sum + (distance >= threshold).astype(jnp.int32)
    return bucket_sum


def running_starts(lengths):
    count = lengths.shape[0]
    order = jnp.arange(count, dtype=jnp.int32)
    earlier = order[None, :] < order[:, None]
    return jnp.sum(jnp.where(earlier, lengths[None, :], 0), axis=1)


def places(initial, lengths):
    starts = running_starts(lengths)
    inside = initial[:, None] >= starts[None, :]
    sequence = jnp.sum(inside.astype(jnp.int32), axis=1) - 1
    opening = jnp.max(jnp.where(inside, starts[None, :], 0), axis=1)
    return (sequence, initial - opening)


def dot(left, right):
    return jnp.dot(left, right, preferred_element_type=F32)


def mat_t(left, right):
    return lax.dot_general(left, right, (((1,), (1,)), ((), ())), preferred_element_type=F32)


def t_mat(left, right):
    return lax.dot_general(left, right, (((0,), (0,)), ((), ())), preferred_element_type=F32)


def norm_back(grad_in, normed, inverse, gain_in):
    scaled = grad_in * gain_in
    return inverse * (scaled - normed * jnp.mean(scaled * normed, axis=-1, keepdims=True))


def pair_terms(table_here, query_seq, query_pos, key_seq, key_pos, key_mask):
    bucket = bucket_of(key_pos[None, :] - query_pos[:, None])
    bucket_ids = jnp.arange(table_here.shape[0], dtype=jnp.int32)
    chosen = bucket[None, :, :, None] == bucket_ids[None, None, None, :]
    table_heads = jnp.transpose(table_here)[:, None, None, :]
    added_terms = jnp.sum(jnp.where(chosen, table_heads, 0.0), axis=-1)
    added_terms = added_terms + key_mask.astype(F32)[None, None, :]
    same_seq = key_seq[None, :] == query_seq[:, None]
    return (added_terms, same_seq, chosen)


def score_block(query_heads, key_heads, added_terms, same_seq):
    raw_score = jnp.einsum("qhd,khd->hqk", query_heads, key_heads, preferred_element_type=F32)
    return jnp.where(same_seq[None], raw_score + added_terms, MASKED)


class General:
    def __init__(self, q, k, v, mask, lengths, table):
        self.tok = q.shape[0]
        self.cols = q.shape[1]
        heads = self.cols // HD
        self.table = table
        n = lax.axis_size("ctx")
        self.all = self.tok * n
        rows = 2 * self.tok
        blocks = self.all // rows
        seq_all, pos_all = places(jnp.arange(self.all, dtype=jnp.int32), lengths)
        first = lax.axis_index("ctx") * self.tok
        self.q_seq = lax.dynamic_slice_in_dim(seq_all, first, self.tok)
        self.q_pos = lax.dynamic_slice_in_dim(pos_all, first, self.tok)
        self.q = q.reshape(self.tok, heads, HD)
        self.blocks = (
            lax.all_gather(k, "ctx", axis=0, tiled=True).reshape(blocks, rows, heads, HD),
            lax.all_gather(v, "ctx", axis=0, tiled=True).reshape(blocks, rows, heads, HD),
            seq_all.reshape(blocks, rows),
            pos_all.reshape(blocks, rows),
            lax.all_gather(mask, "ctx", axis=0, tiled=True).reshape(blocks, rows),
        )
        self.heads = heads

    def forward(self):
        def top_step(state, block):
            top, total = state
            k, _, seq, pos, mask = block
            added, same, _ = pair_terms(self.table, self.q_seq, self.q_pos, seq, pos, mask)
            scores = score_block(self.q, k, added, same)
            new_top = jnp.maximum(top, jnp.max(scores, axis=-1))
            total = total * jnp.exp(top - new_top) + jnp.sum(
                jnp.exp(scores - new_top[..., None]), axis=-1
            )
            return ((new_top, total), None)

        def value_step(out, block):
            high, low = out
            k, v, seq, pos, mask = block
            added, same, _ = pair_terms(self.table, self.q_seq, self.q_pos, seq, pos, mask)
            probs = jnp.exp(score_block(self.q, k, added, same) - self.lse[..., None])
            probs_high = probs.astype(BF16)
            rest = (probs - probs_high.astype(F32)).astype(BF16)
            high = high + jnp.einsum("hqk,khd->qhd", probs_high, v, preferred_element_type=F32)
            low = low + jnp.einsum("hqk,khd->qhd", rest, v, preferred_element_type=F32)
            return ((high, low), None)

        start = (
            jnp.full((self.heads, self.tok), MASKED, F32),
            jnp.zeros((self.heads, self.tok), F32),
        )
        (top, total), _ = lax.scan(top_step, start, self.blocks)
        self.lse = top + jnp.log(total)
        self.zero = jnp.zeros((self.tok, self.heads, HD), F32)
        (high, low), _ = lax.scan(value_step, (self.zero, self.zero), self.blocks)
        self.exact = high + low
        return high.reshape(self.tok, self.cols).astype(BF16)

    def backward(self, do):
        grad = do.reshape(self.tok, self.heads, HD)
        delta = jnp.transpose(jnp.sum(grad.astype(F32) * self.exact, axis=-1))

        def step(state, block):
            q_acc, table_acc = state
            k, v, seq, pos, mask = block
            added, same, chosen = pair_terms(self.table, self.q_seq, self.q_pos, seq, pos, mask)
            probs = jnp.exp(score_block(self.q, k, added, same) - self.lse[..., None])
            dp = jnp.einsum("qhd,khd->hqk", grad, v, preferred_element_type=F32)
            ds = probs * (dp - delta[..., None])
            low = ds.astype(BF16)
            q_acc = q_acc + jnp.einsum("hqk,khd->qhd", low, k, preferred_element_type=F32)
            sums = jnp.sum(jnp.where(chosen, ds[..., None], 0.0), axis=(1, 2))
            emitted = (
                jnp.einsum("hqk,qhd->khd", low, self.q, preferred_element_type=F32),
                jnp.einsum("hqk,qhd->khd", probs.astype(BF16), grad, preferred_element_type=F32),
                jnp.sum(ds, axis=(0, 1)),
            )
            return ((q_acc, table_acc + jnp.transpose(sums)), emitted)

        start = (self.zero, jnp.zeros((self.table.shape[0], self.heads), F32))
        (q_acc, table_acc), (dk, dv, dm) = lax.scan(step, start, self.blocks)
        dk = lax.psum_scatter(
            dk.reshape(self.all, self.cols), "ctx", scatter_dimension=0, tiled=True
        )
        dv = lax.psum_scatter(
            dv.reshape(self.all, self.cols), "ctx", scatter_dimension=0, tiled=True
        )
        dq = q_acc.reshape(self.tok, self.cols)
        return (dq.astype(BF16), dk.astype(BF16), dv.astype(BF16), table_acc, dm.reshape(self.all))


class Halving:
    def __init__(self, width):
        self.n = lax.axis_size("ctx")
        self.bits = self.n.bit_length() - 1
        self.own = width // self.n
        self.rows = -(-self.own // 16) * 16
        places = [int(format(b, f"0{self.bits}b")[::-1], 2) for b in range(self.n)]
        order = jnp.asarray(places, jnp.int32)
        owner = jnp.bitwise_xor(order, lax.axis_index("ctx"))
        inner = jnp.arange(self.rows, dtype=jnp.int32)
        source = jnp.where(inner < self.own, owner[:, None] * self.own + inner, -1).reshape(-1)
        features = jnp.arange(width, dtype=jnp.int32)
        self.select = (features[:, None] == source[None, :]).astype(BF16)

    def arrange(self, x):
        return dot(x, self.select).astype(BF16)

    def scatter(self, left, right):
        half = left.shape[1] // 2
        send = t_mat(left[:, half:], right).astype(BF16)
        keep = t_mat(left[:, :half], right).astype(BF16)
        for bit in range(self.bits):
            pairs = [(i, i ^ (1 << bit)) for i in range(self.n)]
            got = lax.ppermute(send, "ctx", pairs)
            half = half // 2
            if bit == self.bits - 1:
                return keep[: self.own].astype(F32) + got[: self.own].astype(F32)
            send = (keep[half:].astype(F32) + got[half:].astype(F32)).astype(BF16)
            keep = (keep[:half].astype(F32) + got[:half].astype(F32)).astype(BF16)


def general(
    inputs,
    delete_mask,
    lengths,
    dealing,
    w_query,
    w_key,
    w_value,
    w_output,
    bias_table,
    norm_attn,
    w_gate,
    w_up,
    w_down,
    norm_ffn,
    out_grad,
):
    tok = inputs.shape[0]
    width = inputs.shape[1]
    n = lax.axis_size("ctx")
    ctx = lax.axis_index("ctx")
    wt = lax.axis_index("wt")
    tokens_all = tok * n
    cols = w_query.shape[1]
    swap = [(0, 1), (1, 0)]

    def other(x):
        return lax.ppermute(x, "wt", swap)

    sums = Halving(width)
    stream_in = inputs.astype(F32)
    inverse_one = lax.rsqrt(jnp.mean(stream_in * stream_in, axis=-1, keepdims=True) + EPSILON)
    normed_one = stream_in * inverse_one
    hidden_one = (normed_one * norm_attn).astype(BF16)
    attention = General(
        dot(hidden_one, w_query).astype(BF16),
        dot(hidden_one, w_key).astype(BF16),
        dot(hidden_one, w_value).astype(BF16),
        delete_mask,
        lengths,
        bias_table,
    )
    w_output_other = other(w_output)
    arranged_grad = sums.arrange(out_grad)
    arranged_one = sums.arrange(hidden_one)
    inner_grad = mat_t(out_grad, w_down)
    attended = attention.forward()
    branch_attn = dot(attended, w_output) + dot(other(attended), w_output_other)
    stream_mid = stream_in + branch_attn
    inverse_two = lax.rsqrt(jnp.mean(stream_mid * stream_mid, axis=-1, keepdims=True) + EPSILON)
    normed_two = stream_mid * inverse_two
    hidden_two = (normed_two * norm_ffn).astype(BF16)
    gate_value = dot(hidden_two, w_gate)
    up_value = dot(hidden_two, w_up)

    def gated_unit(gate_in, up_in):
        return jax.nn.gelu(gate_in, approximate=True) * up_in

    activated, gated_pull = jax.vjp(gated_unit, gate_value, up_value)
    inner_low = activated.astype(BF16)
    down_part = sums.scatter(arranged_grad, inner_low)
    gate_grad, up_grad = gated_pull(inner_grad)
    gate_low = gate_grad.astype(BF16)
    up_low = up_grad.astype(BF16)
    back_part = (mat_t(gate_low, w_gate) + mat_t(up_low, w_up)).astype(BF16)
    hidden_two_grad = back_part.astype(F32) + other(back_part).astype(F32)
    arranged_two = sums.arrange(hidden_two)
    gate_part = sums.scatter(arranged_two, gate_low)
    up_part = sums.scatter(arranged_two, up_low)
    gain_two_grad = jnp.sum(hidden_two_grad * normed_two, axis=0)
    stream_mid_grad = out_grad.astype(F32) + norm_back(
        hidden_two_grad, normed_two, inverse_two, norm_ffn
    )
    attn_grad_low = stream_mid_grad.astype(BF16)
    attended_grad = mat_t(attn_grad_low, w_output).astype(BF16)
    output_part = sums.scatter(sums.arrange(attn_grad_low), attended)
    ffn_part = dot(inner_low, w_down).astype(BF16)
    branch_ffn = ffn_part.astype(F32) + other(ffn_part).astype(F32)
    stream_out = stream_mid + branch_ffn
    squares = jnp.stack(
        [
            jnp.sum(stream_out * stream_out),
            jnp.sum(branch_attn * branch_attn),
            jnp.sum(branch_ffn * branch_ffn),
        ]
    )
    dq, dk, dv, table_acc, dmask = attention.backward(attended_grad)
    projections = jnp.concatenate([dq, dk, dv], axis=1)
    projection_part = sums.scatter(arranged_one, projections)
    w_all = jnp.concatenate([w_query, w_key, w_value], axis=1)
    one_part = mat_t(projections, w_all).astype(BF16)
    hidden_one_grad = one_part.astype(F32) + other(one_part).astype(F32)
    gain_one_grad = jnp.sum(hidden_one_grad * normed_one, axis=0)
    input_grad = stream_mid_grad + norm_back(hidden_one_grad, normed_one, inverse_one, norm_attn)
    heads = table_acc.shape[1]
    flat = table_acc.reshape(-1)
    table_slots = jnp.where(
        jnp.arange(2)[:, None] == wt, jnp.broadcast_to(flat, (2, flat.shape[0])), 0.0
    ).reshape(-1)
    small = jnp.concatenate(
        [
            dmask,
            table_slots,
            0.5 * gain_one_grad,
            0.5 * gain_two_grad,
            0.5 * squares,
        ]
    )
    small = lax.psum(small, ("ctx", "wt"))
    mask_all = small[:tokens_all].reshape(n, 1, tok)
    base = tokens_all
    table_grad = lax.dynamic_slice_in_dim(small, base + wt * flat.shape[0], flat.shape[0])
    table_grad = table_grad.reshape(-1, heads)
    base += 2 * flat.shape[0]
    own = width // n
    gain_one = lax.dynamic_slice_in_dim(small, base + ctx * own, own)
    gain_two = lax.dynamic_slice_in_dim(small, base + width + ctx * own, own)
    square_sum = small[base + 2 * width :]
    root_means = jnp.sqrt(square_sum / (tokens_all * width))
    quota = tok // n
    slots = lax.dynamic_slice_in_dim(dealing, ctx * tok, tok).reshape(n, quota, 1)
    inside = slots - (jnp.arange(n, dtype=jnp.int32) * tok)[:, None, None]
    chosen = inside == jnp.arange(tok, dtype=jnp.int32)[None, None, :]
    mask_grad = jnp.sum(jnp.where(chosen, mask_all, 0.0), axis=-1).reshape(tok)
    return (
        stream_out.astype(BF16),
        input_grad.astype(BF16),
        mask_grad.astype(BF16),
        projection_part[:, :cols],
        projection_part[:, cols : 2 * cols],
        projection_part[:, 2 * cols :],
        jnp.transpose(output_part),
        table_grad,
        gain_one,
        gate_part,
        up_part,
        jnp.transpose(down_part),
        gain_two,
        root_means,
    )


PER = MIN_LEN // CHUNK
SHIFTS = (-3, -2, -1, 1, 2, 3)
TILE = 256
MESH = pl.DeviceIdType.MESH
GELU = 0.7978845608028654
CUBIC = 0.044715


def iota(shape, axis):
    return lax.broadcasted_iota(jnp.int32, shape, axis)


def head_lanes(shape, head, value_order):
    place = (head + 2 if head < 2 else 1) if value_order else head
    return iota(shape, 1) // HD == place


def holds(device, sequence):
    first = (sequence * PER) // 3
    last = (sequence * PER + PER - 1) // 3
    return jnp.logical_and(device >= first, device <= last)


def inside(device):
    return jnp.logical_and(device >= 0, device < 16)


def flip(index, bit):
    return index + bit * (1 - 2 * ((index // bit) % 2))


def multiple(value, of):
    return value if isinstance(value, int) else pl.multiple_of(value, of)


def copy_to(src, dst, send, recv, ctx, wt):
    return pltpu.make_async_remote_copy(
        src_ref=src,
        dst_ref=dst,
        send_sem=send,
        recv_sem=recv,
        device_id=(ctx, wt),
        device_id_type=MESH,
    )


def row_blocks(width, size=CHUNK):
    return [slice(k, min(k + size, width)) for k in range(0, width, size)]


def announce(ctx, wt, bits):
    barrier = pltpu.get_barrier_semaphore()
    count = 1 + len(bits)
    pl.semaphore_signal(barrier, inc=1, device_id=(ctx, 1 - wt), device_id_type=MESH)
    for bit in bits:
        pl.semaphore_signal(
            barrier, inc=1, device_id=(flip(ctx, bit), wt), device_id_type=MESH
        )
    for shift in SHIFTS:
        peer = ctx + shift

        @pl.when(inside(peer))
        def _():
            pl.semaphore_signal(barrier, inc=1, device_id=(peer, wt), device_id_type=MESH)

        count = count + inside(peer).astype(jnp.int32)
    return barrier, count


def gain_of(params_ref, rows, which):
    row = which * 12 + rows.start // CHUNK
    wide = jnp.broadcast_to(params_ref[row : row + 1, :], (8, CHUNK))
    return jnp.transpose(wide)[: rows.stop - rows.start, 0:1]


def near_fill(table_ref, near_ref):
    bucket = bucket_of(iota((1, 512), 1) - 255)
    for h in range(3):
        row = jnp.zeros((1, 512), F32)
        for b in range(table_ref.shape[1]):
            row = row + jnp.where(bucket == b, table_ref[h : h + 1, b : b + 1], 0.0)
        near_ref[h : h + 1, :] = row


def arrange(src_ref, lhs_ref, half_ref, ctx, own):
    rows = lhs_ref.shape[0] // 8

    def block(b, dst_ref, side):
        owner = ((ctx % 2) + side) % 2
        for k in range(1, 4):
            mine = (ctx // (1 << k)) % 2
            turn = (b // (8 >> k)) % 2
            owner = owner + (mine + turn - 2 * mine * turn) * (1 << k)
        start = owner * own
        base = pl.multiple_of((start // 8) * 8, 8)
        tall = src_ref[pl.ds(base, rows + 8), :]
        tall = jnp.where(start % 8 == 0, tall[:rows], tall[4 : rows + 4])
        dst_ref[pl.ds(pl.multiple_of(b * rows, rows), rows), 0 : src_ref.shape[1]] = tall.astype(
            BF16
        )

    def both(b, carry):
        block(b, lhs_ref, 0)
        block(b, half_ref, 1)
        return carry

    lax.fori_loop(0, 8, both, 0)


def near_tiles(near_ref, tiles_ref):
    for h in range(3):
        wide = jnp.broadcast_to(near_ref[h : h + 1, :], (CHUNK, 512))
        tile = pltpu.roll(wide, 512 - 127, 1, stride=1, stride_axis=0)
        tiles_ref[h] = tile[:, : 3 * CHUNK]


def bias_row(near_ref, tiles_ref, row_ref, h, within):
    lane = iota((1, MIN_LEN + 2 * CHUNK), 1) // CHUNK
    sides = jnp.where(lane < within, near_ref[h : h + 1, 0:1], near_ref[h : h + 1, 510:511])
    row_ref[...] = jnp.broadcast_to(sides, row_ref.shape)
    row_ref[:, pl.ds(pl.multiple_of(within * CHUNK, CHUNK), 3 * CHUNK)] = tiles_ref[h]
    return row_ref[:, CHUNK : CHUNK + MIN_LEN]


def columns_of(dst_ref, base, wq, wk, wv):
    for rows in row_blocks(wq.shape[-1]):
        zero = jnp.zeros((HD, rows.stop - rows.start), BF16)
        dst_ref[base, rows, :] = jnp.transpose(jnp.concatenate([wq[:, rows], zero], 0))
        dst_ref[base + 1, rows, :] = jnp.transpose(
            jnp.concatenate([wk[:, rows], wv[2 * HD : 3 * HD, rows]], 0)
        )
        dst_ref[base + 2, rows, 0 : 2 * HD] = jnp.transpose(wv[0 : 2 * HD, rows])


def front_kernel(
    own,
    xt_ref,
    ogt_ref,
    wq_ref,
    wk_ref,
    wv_ref,
    wo_ref,
    table_ref,
    norms_ref,
    q_ref,
    kv_ref,
    mask_out_ref,
    lse_ref,
    pair_ref,
    mid_ref,
    two_ref,
    og_ref,
    lhs_two_ref,
    lhs_og_ref,
    lhs_one_ref,
    square_ref,
    one_ref,
    tall_ref,
    kvt_ref,
    masks_ref,
    near_ref,
    tiles_ref,
    row_ref,
    other_o_ref,
    other_wo_ref,
    turned_ref,
    half_ref,
    kv_send,
    kv_recv,
    mask_send,
    mask_recv,
    x_send,
    x_recv,
    core_send,
    core_recv,
):
    ctx = lax.axis_index("ctx")
    wt = lax.axis_index("wt")
    width = xt_ref.shape[0]
    tok = xt_ref.shape[1]
    first_seq = (3 * ctx) // PER
    barrier, count = announce(ctx, wt, (1,))

    def over(src, dst, k):
        return copy_to(src, dst, x_send.at[k], x_recv.at[k], ctx, 1 - wt)

    def core(src, dst, k):
        return copy_to(src, dst, core_send.at[k], core_recv.at[k], flip(ctx, 1), wt)

    def mask_copy(k, peer):
        return copy_to(masks_ref.at[len(SHIFTS)], masks_ref.at[k], mask_send.at[k], mask_recv.at[k], peer, wt)

    def kv_copy(k, i, device, peer):
        g = 3 * device + i
        here = pl.multiple_of((g - PER * ((3 * device) // PER)) * CHUNK, CHUNK)
        there = pl.multiple_of((g - PER * ((3 * peer) // PER)) * CHUNK, CHUNK)
        return copy_to(
            kv_ref.at[pl.ds(here, CHUNK), :],
            kv_ref.at[pl.ds(there, CHUNK), :],
            kv_send.at[k, i],
            kv_recv.at[k, i],
            peer,
            wt,
        )

    def moves(device, i, peer):
        return jnp.logical_and(
            holds(peer, (3 * device + i) // PER), jnp.logical_and(inside(device), inside(peer))
        )

    over_wo = over(wo_ref, other_wo_ref, 0)
    over_o = over(pair_ref.at[0:tok, :], other_o_ref, 1)
    core_og = core(half_ref.at[0], lhs_og_ref.at[:, tok : 2 * tok], 0)
    core_one = core(half_ref.at[1], lhs_one_ref.at[:, tok : 2 * tok], 1)
    core_two = core(half_ref.at[2], lhs_two_ref.at[:, tok : 2 * tok], 2)
    core_o = core(pair_ref.at[0:tok, :], pair_ref.at[tok : 2 * tok, :], 3)

    for i in range(3):
        masks_ref[len(SHIFTS), :, i * CHUNK : (i + 1) * CHUNK] = jnp.broadcast_to(
            norms_ref[24 + i : 25 + i, :], (8, CHUNK)
        )
    tall_ref[width:, :] = jnp.zeros((tall_ref.shape[0] - width, tok), F32)
    total = jnp.zeros((1, tok), F32)
    for rows in row_blocks(width):
        x = xt_ref[rows, :].astype(F32)
        total = total + jnp.sum(x * x, axis=0, keepdims=True)
    inverse = lax.rsqrt(total * (1.0 / width) + EPSILON)
    for rows in row_blocks(width):
        h = xt_ref[rows, :].astype(F32) * inverse * gain_of(norms_ref, rows, 0)
        tall_ref[rows, :] = h
        one_ref[rows, :] = h.astype(BF16)
    kt = dot(wk_ref[...], one_ref[...]).astype(BF16)
    vt = dot(wv_ref[...], one_ref[...]).astype(BF16)
    kvt_ref[0 : 3 * HD, :] = kt
    kvt_ref[3 * HD : 4 * HD, :] = vt[2 * HD :, :]
    kvt_ref[4 * HD :, :] = vt[: 2 * HD, :]
    pl.semaphore_wait(barrier, count)
    for k, shift in enumerate(SHIFTS):

        @pl.when(inside(ctx + shift))
        def _():
            mask_copy(k, ctx + shift).start()

    for i in range(3):
        here = pl.multiple_of((3 * ctx + i - PER * first_seq) * CHUNK, CHUNK)
        kv_ref[pl.ds(here, CHUNK), :] = jnp.transpose(kvt_ref[:, i * CHUNK : (i + 1) * CHUNK])
        for k, shift in enumerate(SHIFTS):

            @pl.when(moves(ctx, i, ctx + shift))
            def _():
                kv_copy(k, i, ctx, ctx + shift).start()

    over_wo.start()
    qt = dot(wq_ref[...], one_ref[...]).astype(BF16)
    q_ref[...] = jnp.transpose(jnp.concatenate([qt, jnp.zeros((HD, tok), BF16)], 0))
    arrange(tall_ref, lhs_one_ref, half_ref.at[1], ctx, own)
    core_one.start()
    for rows in row_blocks(width):
        tall_ref[rows, :] = ogt_ref[rows, :].astype(F32)
        og_ref[:, rows] = jnp.transpose(ogt_ref[rows, :])
    arrange(tall_ref, lhs_og_ref, half_ref.at[0], ctx, own)
    core_og.start()
    for rows in row_blocks(width):
        count = rows.stop - rows.start
        turned_ref[0, rows, :] = jnp.transpose(
            jnp.concatenate([wo_ref[:, rows], jnp.zeros((HD, count), BF16)], 0)
        )
    near_fill(table_ref, near_ref)
    near_tiles(near_ref, tiles_ref)

    @pl.when((3 * ctx + 2) // PER == first_seq)
    def _():
        kv_ref[MIN_LEN:, :] = jnp.zeros((MIN_LEN, 6 * HD), BF16)

    for k, shift in enumerate(SHIFTS):
        source = ctx - shift

        @pl.when(inside(source))
        def _():
            mask_copy(k, source).wait_recv()

        for i in range(3):

            @pl.when(moves(source, i, ctx))
            def _():
                g = 3 * source + i
                there = pl.multiple_of((g - PER * first_seq) * CHUNK, CHUNK)
                spot = kv_ref.at[pl.ds(there, CHUNK), :]
                copy_to(spot, spot, kv_send.at[k, i], kv_recv.at[k, i], source, wt).wait_recv()

    for c in range(2 * PER):
        g = PER * first_seq + c
        row = jnp.zeros((1, CHUNK), F32)
        for k, shift in enumerate((*SHIFTS, 0)):
            for i in range(3):
                match = jnp.logical_and(g // 3 == ctx - shift, g % 3 == i)
                row = jnp.where(match, masks_ref[k, 0:1, i * CHUNK : (i + 1) * CHUNK], row)
        mask_out_ref[0:1, c * CHUNK : (c + 1) * CHUNK] = row
    for i in range(3):
        rows = slice(i * CHUNK, (i + 1) * CHUNK)
        g = 3 * ctx + i
        window = pl.multiple_of((g // PER - first_seq) * MIN_LEN, MIN_LEN)
        q = q_ref[rows, :]
        keys = kv_ref[pl.ds(window, MIN_LEN), 0:256]
        values = kv_ref[pl.ds(window, MIN_LEN), 128:384]
        mask = mask_out_ref[:, pl.ds(window, MIN_LEN)]
        out = jnp.zeros((CHUNK, 256), F32)
        lse = jnp.zeros((CHUNK, CHUNK), F32)
        for h in range(3):
            s = mat_t(jnp.where(head_lanes(q.shape, h, False), q, jnp.zeros_like(q)), keys)
            s = s + bias_row(near_ref, tiles_ref, row_ref, h, g % PER) + mask
            top = jnp.max(s, axis=1, keepdims=True)
            e = jnp.exp(s - top)
            sums = jnp.sum(e, axis=1, keepdims=True)
            p = (e * (1.0 / sums)).astype(BF16)
            out = jnp.where(head_lanes(out.shape, h, True), dot(p, values), out)
            lse = jnp.where(iota(lse.shape, 1) == h, top + jnp.log(sums), lse)
        late = pltpu.roll(out[:, 0:128], HD, 1)
        late = jnp.where(iota(late.shape, 1) < HD, late, 0.0)
        pair_ref[rows, 0:128] = out[:, 128:256].astype(BF16)
        pair_ref[rows, 128:256] = late.astype(BF16)
        lse_ref[rows, :] = lse
    over_o.start()
    core_o.start()
    over_wo.wait_recv()
    for rows in row_blocks(width):
        count = rows.stop - rows.start
        turned_ref[1, rows, :] = jnp.transpose(
            jnp.concatenate([other_wo_ref[:, rows], jnp.zeros((HD, count), BF16)], 0)
        )
    over_o.wait_recv()
    total = jnp.zeros((1, tok), F32)
    squares = jnp.zeros((1, tok), F32)
    for rows in row_blocks(width, 368):
        branch = mat_t(turned_ref[0, rows, :], pair_ref[0:tok, :]) + mat_t(
            turned_ref[1, rows, :], other_o_ref[...]
        )
        mid = xt_ref[rows, :].astype(F32) + branch
        mid_ref[rows, :] = mid
        total = total + jnp.sum(mid * mid, axis=0, keepdims=True)
        squares = squares + jnp.sum(branch * branch, axis=0, keepdims=True)
    square_ref[...] = jnp.broadcast_to(jnp.sum(squares, axis=1, keepdims=True), square_ref.shape)
    inverse = lax.rsqrt(total * (1.0 / width) + EPSILON)
    for rows in row_blocks(width):
        h = mid_ref[rows, :] * inverse * gain_of(norms_ref, rows, 1)
        tall_ref[rows, :] = h
        two_ref[:, rows] = jnp.transpose(h.astype(BF16))
    arrange(tall_ref, lhs_two_ref, half_ref.at[2], ctx, own)
    core_two.start()
    for each in (core_og, core_one, core_o, core_two):
        each.wait()
    for each in (over_wo, over_o):
        each.wait_send()
    for k, shift in enumerate(SHIFTS):

        @pl.when(inside(ctx + shift))
        def _():
            mask_copy(k, ctx + shift).wait_send()

        for i in range(3):

            @pl.when(moves(ctx, i, ctx + shift))
            def _():
                kv_copy(k, i, ctx, ctx + shift).wait_send()


def in_vmem():
    return pl.BlockSpec(memory_space=pltpu.VMEM)


def anywhere():
    return pl.BlockSpec(memory_space=pl.ANY)


def shape_of(shape, dtype):
    return jax.ShapeDtypeStruct(shape, dtype)


def front(xt, ogt, wq, wk, wv, wo, table, params):
    width, tok = xt.shape
    own = width // 16
    rows = 8 * (-(-own // 16) * 16)
    out_shape = (
        shape_of((tok, 256), BF16),
        shape_of((2 * MIN_LEN, 384), BF16),
        shape_of((1, 2 * MIN_LEN), F32),
        shape_of((tok, CHUNK), F32),
        shape_of((2 * tok, 256), BF16),
        shape_of((width, tok), F32),
        shape_of((tok, width), BF16),
        shape_of((tok, width), BF16),
        shape_of((rows, 2 * tok), BF16),
        shape_of((rows, 2 * tok), BF16),
        shape_of((rows, 2 * tok), BF16),
        shape_of((8, CHUNK), F32),
    )
    dma = pltpu.SemaphoreType.DMA
    return pl.pallas_call(
        partial(front_kernel, own),
        out_shape=out_shape,
        in_specs=[in_vmem()] * 8,
        out_specs=(in_vmem(),) * len(out_shape),
        scratch_shapes=[
            pltpu.VMEM((width, tok), BF16),
            pltpu.VMEM((width + 16, tok), F32),
            pltpu.VMEM((384, tok), BF16),
            pltpu.VMEM((len(SHIFTS) + 1, 8, tok), F32),
            pltpu.VMEM((8, 512), F32),
            pltpu.VMEM((3, CHUNK, 3 * CHUNK), F32),
            pltpu.VMEM((CHUNK, MIN_LEN + 2 * CHUNK), F32),
            pltpu.VMEM((tok, 256), BF16),
            pltpu.VMEM((192, width), BF16),
            pltpu.VMEM((2, width, 256), BF16),
            pltpu.VMEM((3, rows, tok), BF16),
            dma((len(SHIFTS), 3)),
            dma((len(SHIFTS), 3)),
            dma((len(SHIFTS),)),
            dma((len(SHIFTS),)),
            dma((2,)),
            dma((2,)),
            dma((4,)),
            dma((4,)),
        ],
        compiler_params=pltpu.CompilerParams(
            collective_id=1, has_side_effects=True, vmem_limit_bytes=56 << 20
        ),
        cost_estimate=pl.CostEstimate(
            flops=8 * tok * width * 640, bytes_accessed=20 << 20, transcendentals=3 << 20
        ),
        name="front",
    )(xt, ogt, wq, wk, wv, wo, table, params)


GROUPS = 7
TILES = 24
SMALL = 112
NEAR_ROW, FAR_ROW, TWO_ROW, ONE_ROW, SQUARE_ROW = 56, 68, 80, 96, 108
RING = 6
AHEAD = 3


def back_kernel(
    own,
    two_ref,
    og_ref,
    mid_ref,
    norms_ref,
    q_ref,
    lse_ref,
    pair_ref,
    wo_ref,
    wq_ref,
    wk_ref,
    wv_ref,
    mask_ref,
    table_ref,
    square_ref,
    gate_hbm,
    up_hbm,
    down_hbm,
    lhs_two_hbm,
    lhs_og_hbm,
    lhs_one_hbm,
    kv_hbm,
    ogt_hbm,
    xt_hbm,
    down_out,
    gate_out,
    up_out,
    tail_out,
    y_out,
    dx_out,
    small_ref,
    lhs_two_ref,
    lhs_og_ref,
    keep_ref,
    rhs_ref,
    first_ref,
    second_ref,
    third_ref,
    stream_ref,
    grad_ref,
    acc_ref,
    over_ref,
    got_ref,
    side_ref,
    kv_ref,
    back_ref,
    near_ref,
    tiles_ref,
    pad_ref,
    diag_ref,
    dqkv_ref,
    lhs_da_ref,
    half_ref,
    other_w_ref,
    small_got_ref,
    step_send,
    step_recv,
    rhs_send,
    rhs_recv,
    free_sem,
    load_sem,
    local_sem,
    x_send,
    x_recv,
    back_send,
    back_recv,
    core_send,
    core_recv,
    small_send,
    small_recv,
):
    ctx = lax.axis_index("ctx")
    wt = lax.axis_index("wt")
    width, tok = mid_ref.shape
    first_seq = (3 * ctx) // PER
    blocks = row_blocks(width)
    barrier, count = announce(ctx, wt, (1, 2, 4, 8))

    def over(src, dst, k):
        return copy_to(src, dst, x_send.at[k], x_recv.at[k], ctx, 1 - wt)

    def core(src, dst, k):
        return copy_to(src, dst, core_send.at[k], core_recv.at[k], flip(ctx, 1), wt)

    over_w = [over(w, other_w_ref.at[k], k) for k, w in enumerate((wq_ref, wk_ref, wv_ref))]
    over_two = over(over_ref.at[0], got_ref.at[0], 3)
    over_f = over(over_ref.at[1], got_ref.at[1], 4)
    over_dqkv = over(dqkv_ref.at[0], dqkv_ref.at[1], 5)
    core_da = core(half_ref, lhs_da_ref.at[:, tok : 2 * tok], 0)
    load_kv = pltpu.make_async_copy(kv_hbm, kv_ref, local_sem.at[0])
    load_og = pltpu.make_async_copy(ogt_hbm, side_ref, local_sem.at[1])
    load_x = pltpu.make_async_copy(xt_hbm, side_ref, local_sem.at[2])
    load_left = (
        pltpu.make_async_copy(lhs_two_hbm, lhs_two_ref, local_sem.at[3]),
        pltpu.make_async_copy(lhs_og_hbm, lhs_og_ref, local_sem.at[4]),
    )
    load_one = pltpu.make_async_copy(lhs_one_hbm, lhs_og_ref, local_sem.at[5])
    save_y = pltpu.make_async_copy(got_ref.at[1], y_out, local_sem.at[6])
    save_dx = pltpu.make_async_copy(got_ref.at[0], dx_out, local_sem.at[7])

    def load(j, m):
        slot = j % 2
        source = (gate_hbm, up_hbm, down_hbm)[m]
        return pltpu.make_async_copy(
            source.at[:, pl.ds(multiple(j * TILE, TILE), TILE)],
            stream_ref.at[slot * 3 + m],
            load_sem.at[slot, m],
        )

    def step_copy(s, t):
        bit = (2, 4, 8)[s]
        low, high = ((384, 768), (192, 384), (96, 192))[s]
        return copy_to(
            keep_ref.at[t, low:high, :],
            (first_ref, second_ref, third_ref)[s].at[t],
            step_send.at[s, t],
            step_recv.at[s, t],
            flip(ctx, bit),
            wt,
        )

    def add_in(s, t):
        rows = (384, 192)[s]
        got = (first_ref, second_ref)[s]
        step_copy(s, t).wait_recv()
        total = keep_ref[t, 0:rows, :].astype(F32) + got[t].astype(F32)
        keep_ref[t, 0:rows, :] = total.astype(BF16)

    def finish(t):
        step_copy(2, t).wait_recv()
        total = keep_ref[t, 0:96, :].astype(F32) + third_ref[t].astype(F32)
        if isinstance(t, int) and t >= 3 * GROUPS:
            tail_out[:, (t - 3 * GROUPS) * TILE : (t - 3 * GROUPS + 1) * TILE] = total
            return
        lanes = pl.ds(multiple((t // 3) * TILE, TILE), TILE)
        for m, out in enumerate((down_out, gate_out, up_out)):

            def write(out=out):
                out[:, lanes] = total[0:own]

            if isinstance(t, int):
                if t % 3 == m:
                    write()
            else:
                pl.when(t % 3 == m)(write)

    def when(condition, do):
        if isinstance(condition, bool):
            if condition:
                do()
        else:
            pl.when(condition)(do)

    def step(k, last=3 * GROUPS):
        def second():
            add_in(0, k)
            step_copy(1, k).start()

        def third():
            add_in(1, k - 1)
            step_copy(2, k - 1).start()

        when(k + AHEAD < last, lambda: step_copy(0, k + AHEAD).start())
        when(k < TILES, second)
        if not isinstance(k, int):
            when(k >= 1, third)
        elif 1 <= k <= TILES:
            third()
        when(k >= 2, lambda: finish(k - 2))

    def rhs_copy(slot):
        return copy_to(
            rhs_ref.at[slot, 0:tok, :],
            rhs_ref.at[slot, tok : 2 * tok, :],
            rhs_send.at[slot],
            rhs_recv.at[slot],
            flip(ctx, 1),
            wt,
        )

    def credit():
        pl.semaphore_signal(free_sem, inc=1, device_id=(flip(ctx, 1), wt), device_id_type=MESH)

    def products(j):
        for m in range(3):
            slot = (j % 2) * 3 + m
            rhs_copy(slot).wait_recv()
            lhs = lhs_og_ref if m == 0 else lhs_two_ref
            keep_ref[3 * j + m] = dot(lhs[...], rhs_ref[slot]).astype(BF16)

    def reuse_slots(j):
        for m in range(3):
            rhs_copy((j % 2) * 3 + m).wait_send()
        pl.semaphore_wait(free_sem, 1)

    for m in range(3):
        load(0, m).start()
    for each in load_left:
        each.start()
    load_kv.start()
    load_og.start()
    grad_ref[...] = jnp.zeros_like(grad_ref)
    acc_ref[...] = jnp.zeros_like(acc_ref)
    pl.semaphore_wait(barrier, count)
    for each in over_w:
        each.start()

    def group(j, carry):
        slot = (j % 2) * 3
        for m in range(3):
            load(j, m).wait()

        @pl.when(j < GROUPS - 1)
        def _():
            for m in range(3):
                load(j + 1, m).start()

        @pl.when(j >= 2)
        def _():
            reuse_slots(j)

        gate = dot(two_ref[...], stream_ref[slot])
        up = dot(two_ref[...], stream_ref[slot + 1])
        dhid = dot(og_ref[...], stream_ref[slot + 2])
        square = gate * gate
        bend = jnp.tanh(GELU * gate * (1.0 + CUBIC * square))
        half = 0.5 * (1.0 + bend)
        unit = gate * half
        slope = half + (0.5 * GELU) * gate * (1.0 - bend * bend) * (1.0 + 3.0 * CUBIC * square)
        rhs_ref[slot, 0:tok, :] = (unit * up).astype(BF16)
        rhs_ref[slot + 1, 0:tok, :] = (dhid * up * slope).astype(BF16)
        rhs_ref[slot + 2, 0:tok, :] = (dhid * unit).astype(BF16)
        for m in range(3):
            rhs_copy(slot + m).start()

        @pl.when(j == 1)
        def _():
            for each in load_left:
                each.wait()

        @pl.when(j >= 1)
        def _():
            products(j - 1)
            credit()

        @pl.when(j == 1)
        def _():
            for t in range(AHEAD):
                step_copy(0, t).start()

        pl.when(j == 2)(lambda: step(0))
        pl.when(j >= 3)(lambda: step(2 * j - 5))
        for rows in row_blocks(width, 368):
            grad_ref[rows, :] += mat_t(stream_ref[slot + 1, rows, :], rhs_ref[slot + 2, 0:tok, :]) + mat_t(
                stream_ref[slot, rows, :], rhs_ref[slot + 1, 0:tok, :]
            )
            acc_ref[rows, :] += mat_t(stream_ref[slot + 2, rows, :], rhs_ref[slot, 0:tok, :])
        pl.when(j >= 3)(lambda: step(2 * j - 4))
        return carry

    lax.fori_loop(0, GROUPS, group, 0)
    for rows in blocks:
        over_ref[0, rows, :] = grad_ref[rows, :].astype(BF16)
    for each in over_w:
        each.wait_recv()
    over_two.start()
    for rows in blocks:
        over_ref[1, rows, :] = acc_ref[rows, :].astype(BF16)
    products(GROUPS - 1)
    load_one.start()
    columns_of(stream_ref, 0, wq_ref, wk_ref, wv_ref)
    columns_of(stream_ref, 3, other_w_ref.at[0], other_w_ref.at[1], other_w_ref.at[2])
    acc_ref[...] = jnp.zeros_like(acc_ref)
    small_ref[...] = jnp.zeros_like(small_ref)
    diag_ref[...] = jnp.zeros_like(diag_ref)
    near_fill(table_ref, near_ref)
    near_tiles(near_ref, tiles_ref)
    total = jnp.zeros((1, tok), F32)
    for rows in blocks:
        total = total + jnp.sum(mid_ref[rows, :] * mid_ref[rows, :], axis=0, keepdims=True)
    inverse = lax.rsqrt(total * (1.0 / width) + EPSILON)
    for k in range(9, 16):
        step(k)

    def lane_sums(x, row, rows):
        folded = x[:, 0:128] + x[:, 128:256] + x[:, 256:384]
        place = rows.start // CHUNK
        count = rows.stop - rows.start
        small_ref[row + place : row + place + 1, 0:count] = jnp.sum(
            jnp.transpose(folded), axis=0, keepdims=True
        )

    over_two.wait()
    over_f.start()
    mean = jnp.zeros((1, tok), F32)
    for rows in blocks:
        d = over_ref[0, rows, :].astype(F32) + got_ref[0, rows, :].astype(F32)
        normed = mid_ref[rows, :] * inverse
        lane_sums(d * normed, TWO_ROW, rows)
        d = d * gain_of(norms_ref, rows, 1)
        grad_ref[rows, :] = d
        mean = mean + jnp.sum(d * normed, axis=0, keepdims=True)
    mean = mean * (1.0 / width)
    load_og.wait()
    for rows in blocks:
        normed = mid_ref[rows, :] * inverse
        d = side_ref[rows, :].astype(F32) + inverse * (grad_ref[rows, :] - normed * mean)
        grad_ref[rows, :] = d
        over_ref[0, rows, :] = d.astype(BF16)
    load_x.start()
    dotted = dot(wo_ref[...], over_ref[0]).astype(BF16)
    turned = jnp.transpose(
        jnp.concatenate([jnp.zeros((HD, tok), BF16), dotted[2 * HD :], dotted[: 2 * HD]], 0)
    )
    dqkv_ref[0, :, 0:256] = turned
    arrange(grad_ref, lhs_da_ref, half_ref, ctx, own)
    core_da.start()
    load_kv.wait()
    step(16)

    far = [jnp.zeros((1, MIN_LEN), F32) for _ in range(6)]
    for i in range(3):
        rows = slice(i * CHUNK, (i + 1) * CHUNK)
        g = 3 * ctx + i
        within = g % PER
        window = pl.multiple_of((g // PER - first_seq) * MIN_LEN, MIN_LEN)
        q = q_ref[rows, :]
        do = dqkv_ref[0, rows, 0:256]
        keys = kv_ref[pl.ds(window, MIN_LEN), 0:256]
        values = kv_ref[pl.ds(window, MIN_LEN), 128:384]
        mask = mask_ref[:, pl.ds(window, MIN_LEN)]
        column = iota((1, MIN_LEN), 1) // CHUNK
        dq = jnp.zeros((CHUNK, 256), F32)
        dmask = jnp.zeros((1, MIN_LEN), F32)
        for h in range(3):
            qm = jnp.where(head_lanes(q.shape, h, False), q, jnp.zeros_like(q))
            dom = jnp.where(head_lanes(do.shape, h, True), do, jnp.zeros_like(do))
            s = mat_t(qm, keys) + bias_row(near_ref, tiles_ref, pad_ref, h, within) + mask
            p = jnp.exp(s - lse_ref[rows, h : h + 1])
            dp = mat_t(dom, values)
            delta = jnp.sum(p * dp, axis=1, keepdims=True)
            ds = p * (dp - delta)
            low = ds.astype(BF16)
            dq = jnp.where(head_lanes(dq.shape, h, False), dot(low, keys), dq)
            acc_ref[pl.ds(window, MIN_LEN), 0:256] += t_mat(low, qm)
            acc_ref[pl.ds(window, MIN_LEN), 128:384] += t_mat(p.astype(BF16), dom)
            sums = jnp.sum(ds, axis=0, keepdims=True)
            dmask = dmask + sums
            far[2 * h] = far[2 * h] + jnp.where(column < within - 1, sums, 0.0)
            far[2 * h + 1] = far[2 * h + 1] + jnp.where(column > within + 1, sums, 0.0)
            pad_ref[:, 0:CHUNK] = jnp.zeros((CHUNK, CHUNK), F32)
            pad_ref[:, CHUNK : CHUNK + MIN_LEN] = ds
            pad_ref[:, MIN_LEN + CHUNK :] = jnp.zeros((CHUNK, CHUNK), F32)
            near = pl.multiple_of(within * CHUNK, CHUNK)
            diag_ref[h, :, 0 : 3 * CHUNK] += pad_ref[:, pl.ds(near, 3 * CHUNK)]
        dqkv_ref[0, rows, 0:256] = dq.astype(BF16)
        spots = pl.ds(pl.multiple_of((g // PER) * PER, PER), PER)
        small_ref[spots, :] += jnp.concatenate(
            [dmask[:, c * CHUNK : (c + 1) * CHUNK] for c in range(PER)], 0
        )
        step(17 + i)

    def back_copy(k, i, sender, owner):
        g = 3 * owner + i
        spot = pl.multiple_of((g - PER * ((3 * sender) // PER)) * CHUNK, CHUNK)
        return copy_to(
            kv_ref.at[pl.ds(spot, CHUNK), :],
            back_ref.at[k, i],
            back_send.at[k, i],
            back_recv.at[k, i],
            owner,
            wt,
        )

    def moves(sender, i, owner):
        return jnp.logical_and(
            holds(sender, (3 * owner + i) // PER),
            jnp.logical_and(inside(sender), inside(owner)),
        )

    kv_ref[...] = acc_ref[...].astype(BF16)
    for k, shift in enumerate(SHIFTS):
        for i in range(3):

            @pl.when(moves(ctx, i, ctx + shift))
            def _():
                back_copy(k, i, ctx, ctx + shift).start()

    for h in range(3):
        tile = diag_ref[h]
        count = CHUNK
        while count > 1:
            count //= 2
            tile = tile[:count] + pltpu.roll(tile[count:], 512 - count, 1)
        for c in range(4):
            row = NEAR_ROW + 4 * h + c
            small_ref[row : row + 1, :] = tile[:, c * CHUNK : (c + 1) * CHUNK]
        for side in range(2):
            row = FAR_ROW + 2 * h + side
            small_ref[row : row + 1, :] = jnp.broadcast_to(
                jnp.sum(far[2 * h + side], axis=1, keepdims=True), (1, CHUNK)
            )
    def doubling(r, low, high, slot):
        peer = (flip(ctx, 1 << r), wt) if r < 4 else (ctx, 1 - wt)
        return copy_to(
            small_ref.at[low:high, :],
            small_got_ref.at[slot, 0 : high - low, :],
            small_send.at[slot],
            small_recv.at[slot],
            *peer,
        )

    def doubled(r, low, high, slot):
        doubling(r, low, high, slot).wait()
        small_ref[low:high, :] = small_ref[low:high, :] + small_got_ref[slot, 0 : high - low, :]

    def early(r):
        high = ONE_ROW if r < 4 else NEAR_ROW
        doubling(r, 0, high, r).start()
        if r == 0:
            step(20)
        doubled(r, 0, high, r)

    early(0)
    early(1)
    first = pl.multiple_of((3 * ctx - PER * first_seq) * CHUNK, CHUNK)
    for k, shift in enumerate(SHIFTS):
        for i in range(3):

            @pl.when(moves(ctx - shift, i, ctx))
            def _():
                spot = kv_ref.at[pl.ds(first, CHUNK), :]
                copy_to(
                    spot, back_ref.at[k, i], back_send.at[k, i], back_recv.at[k, i], ctx - shift, wt
                ).wait_recv()
                place = pl.multiple_of(first + i * CHUNK, CHUNK)
                acc_ref[pl.ds(place, CHUNK), :] += back_ref[k, i].astype(F32)

    dqkv_ref[0, :, 256:640] = acc_ref[pl.ds(first, tok), :].astype(BF16)
    over_dqkv.start()

    reuse_slots(GROUPS)
    rhs_ref[3, 0:tok, :] = dqkv_ref[0, :, 0:256]
    rhs_ref[4, 0:tok, :] = dqkv_ref[0, :, 256:512]
    rhs_ref[5, 0:tok, 0:128] = dqkv_ref[0, :, 512:640]
    rhs_ref[5, 0:tok, 128:256] = jnp.zeros((tok, 128), BF16)
    for m in range(3):
        rhs_copy(3 + m).start()
    core_da.wait()
    load_one.wait()
    zero = jnp.zeros((2 * tok, 128), BF16)
    late = pltpu.roll(pair_ref[:, 128:256].astype(F32), HD, 1).astype(BF16)
    extra = (jnp.concatenate([zero, late], 1), None, jnp.concatenate([zero, pair_ref[:, 0:128]], 1))
    for m in range(3):
        rhs_copy(3 + m).wait_recv()
        result = dot(lhs_og_ref[...], rhs_ref[3 + m])
        if extra[m] is not None:
            result = result + dot(lhs_da_ref[...], extra[m])
        keep_ref[3 * GROUPS + m] = result.astype(BF16)
        step_copy(0, 3 * GROUPS + m).start()
    for r in range(2, 5):
        early(r)

    over_dqkv.wait_recv()
    load_x.wait()
    total = jnp.zeros((1, tok), F32)
    for rows in blocks:
        x = side_ref[rows, :].astype(F32)
        total = total + jnp.sum(x * x, axis=0, keepdims=True)
    inverse = lax.rsqrt(total * (1.0 / width) + EPSILON)
    mean = jnp.zeros((1, tok), F32)
    for part in row_blocks(width, 368):
        sides = []
        for turn in range(2):
            side = (wt + turn) % 2
            sides.append(
                mat_t(stream_ref[3 * side, part, :], dqkv_ref[side, :, 0:256])
                + mat_t(stream_ref[3 * side + 1, part, :], dqkv_ref[side, :, 256:512])
                + mat_t(stream_ref[3 * side + 2, part, 0:128], dqkv_ref[side, :, 512:640])
            )
        acc_ref[part, :] = sides[0] + sides[1]
    for rows in blocks:
        d = acc_ref[rows, :]
        normed = side_ref[rows, :].astype(F32) * inverse
        lane_sums(d * normed, ONE_ROW, rows)
        d = d * gain_of(norms_ref, rows, 0)
        acc_ref[rows, :] = d
        mean = mean + jnp.sum(d * normed, axis=0, keepdims=True)
    mean = mean * (1.0 / width)
    for rows in blocks:
        normed = side_ref[rows, :].astype(F32) * inverse
        d = grad_ref[rows, :] + inverse * (acc_ref[rows, :] - normed * mean)
        got_ref[0, rows, :] = d.astype(BF16)
    save_dx.start()
    step(21)

    over_f.wait()
    y_sum = jnp.zeros((1, tok), F32)
    f_sum = jnp.zeros((1, tok), F32)
    for rows in blocks:
        f = over_ref[1, rows, :].astype(F32) + got_ref[1, rows, :].astype(F32)
        y = mid_ref[rows, :] + f
        got_ref[1, rows, :] = y.astype(BF16)
        y_sum = y_sum + jnp.sum(y * y, axis=0, keepdims=True)
        f_sum = f_sum + jnp.sum(f * f, axis=0, keepdims=True)
    save_y.start()
    for k, sums in enumerate((y_sum, f_sum)):
        row = SQUARE_ROW + 2 * k
        small_ref[row : row + 1, :] = jnp.broadcast_to(
            jnp.sum(sums, axis=1, keepdims=True), (1, CHUNK)
        )
    small_ref[SQUARE_ROW + 1 : SQUARE_ROW + 2, :] = square_ref[0:1, :]

    for r in range(4):
        doubling(r, ONE_ROW, SMALL, 5 + r).start()
        step(22 + r)
        doubled(r, ONE_ROW, SMALL, 5 + r)

    for t in range(TILES):
        for s in range(3):
            step_copy(s, t).wait_send()
    for slot in range(RING):
        rhs_copy(slot).wait_send()
    save_y.wait()
    save_dx.wait()
    over_dqkv.wait_send()
    for each in over_w:
        each.wait_send()
    for k, shift in enumerate(SHIFTS):
        for i in range(3):

            @pl.when(moves(ctx, i, ctx + shift))
            def _():
                back_copy(k, i, ctx, ctx + shift).wait_send()


def back(inputs_here, own):
    width, tok = inputs_here[2].shape
    rows = 8 * (-(-own // 16) * 16)
    hidden = inputs_here[14].shape[1]
    out_shape = (
        shape_of((own, hidden), F32),
        shape_of((own, hidden), F32),
        shape_of((own, hidden), F32),
        shape_of((rows // 8, 3 * TILE), F32),
        shape_of((width, tok), BF16),
        shape_of((width, tok), BF16),
        shape_of((SMALL, CHUNK), F32),
    )
    dma = pltpu.SemaphoreType.DMA
    return pl.pallas_call(
        partial(back_kernel, own),
        out_shape=out_shape,
        in_specs=[in_vmem()] * 14 + [anywhere()] * 9,
        out_specs=(in_vmem(),) * 4 + (anywhere(),) * 2 + (in_vmem(),),
        scratch_shapes=[
            pltpu.VMEM((rows, 2 * tok), BF16),
            pltpu.VMEM((rows, 2 * tok), BF16),
            pltpu.VMEM((TILES, rows, TILE), BF16),
            pltpu.VMEM((RING, 2 * tok, TILE), BF16),
            pltpu.VMEM((TILES, rows // 2, TILE), BF16),
            pltpu.VMEM((TILES, rows // 4, TILE), BF16),
            pltpu.VMEM((TILES, rows // 8, TILE), BF16),
            pltpu.VMEM((6, width, TILE), BF16),
            pltpu.VMEM((width + 16, tok), F32),
            pltpu.VMEM((2 * MIN_LEN, tok), F32),
            pltpu.VMEM((2, width, tok), BF16),
            pltpu.VMEM((2, width, tok), BF16),
            pltpu.VMEM((width, tok), BF16),
            pltpu.VMEM((2 * MIN_LEN, 384), BF16),
            pltpu.VMEM((len(SHIFTS), 3, CHUNK, 384), BF16),
            pltpu.VMEM((8, 512), F32),
            pltpu.VMEM((3, CHUNK, 3 * CHUNK), F32),
            pltpu.VMEM((CHUNK, MIN_LEN + 2 * CHUNK), F32),
            pltpu.VMEM((3, CHUNK, 512), F32),
            pltpu.VMEM((2, tok, 640), BF16),
            pltpu.VMEM((rows, 2 * tok), BF16),
            pltpu.VMEM((rows, tok), BF16),
            pltpu.VMEM((3, 192, width), BF16),
            pltpu.VMEM((9, 96, CHUNK), F32),
            dma((3, TILES)),
            dma((3, TILES)),
            dma((RING,)),
            dma((RING,)),
            pltpu.SemaphoreType.REGULAR,
            dma((2, 3)),
            dma((8,)),
            dma((6,)),
            dma((6,)),
            dma((len(SHIFTS), 3)),
            dma((len(SHIFTS), 3)),
            dma((1,)),
            dma((1,)),
            dma((9,)),
            dma((9,)),
        ],
        compiler_params=pltpu.CompilerParams(
            collective_id=2, has_side_effects=True, vmem_limit_bytes=64 << 20
        ),
        cost_estimate=pl.CostEstimate(
            flops=20 * 10**9, bytes_accessed=40 << 20, transcendentals=8 << 20
        ),
        name="back",
    )(*inputs_here)


def finish_kernel(
    small_ref,
    tail_ref,
    dealing_ref,
    down_hbm,
    gate_hbm,
    up_hbm,
    y_hbm,
    dx_hbm,
    down_out,
    gate_out,
    up_out,
    y_out,
    dx_out,
    mask_out,
    query_out,
    key_out,
    value_out,
    output_out,
    table_out,
    one_out,
    two_out,
    root_out,
    sems,
):
    ctx = lax.axis_index("ctx")
    own = query_out.shape[0]
    moves = [
        pltpu.make_async_copy(source, target, sems.at[k])
        for k, (source, target) in enumerate(
            (
                (down_hbm, down_out),
                (gate_hbm, gate_out),
                (up_hbm, up_out),
                (y_hbm, y_out),
                (dx_hbm, dx_out),
            )
        )
    ]
    for each in moves:
        each.start()
    query_out[...] = tail_ref[:own, 0:192]
    key_out[...] = tail_ref[:own, 256:448]
    value_out[:, 0:128] = tail_ref[:own, 512:640]
    value_out[:, 128:192] = tail_ref[:own, 448:512]
    output_out[0:128, :] = jnp.transpose(tail_ref[:, 640:768])[:, :own]
    output_out[128:192, :] = jnp.transpose(tail_ref[:, 128:256])[HD:, :own]
    values = small_ref[0:48, :].astype(BF16)
    for i in range(3):
        mine = iota((48, CHUNK), 0) == 3 * ctx + i
        token = jnp.sum(jnp.where(mine, dealing_ref[...], 0), axis=0, keepdims=True)
        lane = jnp.bitwise_and(token, CHUNK - 1)
        pick = (iota((CHUNK, CHUNK), 0) == lane).astype(F32).astype(BF16)
        found = dot(values, pick)
        row = jnp.right_shift(token, 7)
        mask_out[:, i * CHUNK : (i + 1) * CHUNK] = jnp.sum(
            jnp.where(iota((48, CHUNK), 0) == row, found, 0.0), axis=0, keepdims=True
        ).astype(BF16)
    columns = jnp.transpose(small_ref[NEAR_ROW : NEAR_ROW + 16, :])
    lane = iota((1, CHUNK), 1)
    for h in range(3):
        total = jnp.where(lane == 15, small_ref[FAR_ROW + 2 * h : FAR_ROW + 2 * h + 1, :], 0.0)
        total = total + jnp.where(
            lane == 31, small_ref[FAR_ROW + 2 * h + 1 : FAR_ROW + 2 * h + 2, :], 0.0
        )
        for c in range(4):
            entry = iota((CHUNK, 1), 0) + c * CHUNK
            bucket = bucket_of(jnp.where(entry < 3 * CHUNK, entry, entry - 512) - CHUNK)
            column = columns[:, 4 * h + c : 4 * h + c + 1]
            total = total + jnp.sum(
                jnp.where(bucket == iota((CHUNK, CHUNK), 1), column, 0.0), axis=0, keepdims=True
            )
        table_out[h : h + 1, :] = total[:, : table_out.shape[1]]
    shift = lax.rem(12 * CHUNK - own * ctx, 12 * CHUNK)
    for first, out in ((ONE_ROW, one_out), (TWO_ROW, two_out)):
        row = jnp.concatenate([small_ref[first + k : first + k + 1, :] for k in range(12)], 1)
        turned = pltpu.roll(jnp.broadcast_to(row, (8, 12 * CHUNK)), shift, 1)
        out[...] = turned[0:1, :own]
    scale = 1.0 / (16 * 3 * CHUNK * y_hbm.shape[0])
    square = small_ref[SQUARE_ROW : SQUARE_ROW + 3, :] * scale
    roots = jnp.sqrt(square)
    lane = iota((1, CHUNK), 1)
    row = jnp.where(lane == 0, roots[0:1], jnp.where(lane == 1, roots[1:2], roots[2:3]))
    root_out[...] = row[:, 0:3]
    for each in moves:
        each.wait()


def finish(small, tail, dealing, own, grads, rows):
    hidden = grads[0].shape[1]
    width, tok = rows[0].shape
    return pl.pallas_call(
        finish_kernel,
        out_shape=(
            *(shape_of((own, hidden), F32),) * 3,
            *(shape_of((width, tok), BF16),) * 2,
            shape_of((1, tok), BF16),
            *(shape_of((own, 192), F32),) * 3,
            shape_of((192, own), F32),
            shape_of((3, 32), F32),
            shape_of((1, own), F32),
            shape_of((1, own), F32),
            shape_of((1, 3), F32),
        ),
        in_specs=[in_vmem()] * 8,
        out_specs=(anywhere(),) * 5 + (in_vmem(),) * 9,
        scratch_shapes=[pltpu.SemaphoreType.DMA((5,))],
        compiler_params=pltpu.CompilerParams(vmem_limit_bytes=62 << 20),
        name="finish",
    )(small, tail, dealing, *grads, *rows)


def even(
    inputs,
    delete_mask,
    lengths,
    dealing,
    w_query,
    w_key,
    w_value,
    w_output,
    bias_table,
    norm_attn,
    w_gate,
    w_up,
    w_down,
    norm_ffn,
    out_grad,
):
    tok, width = inputs.shape
    n = lax.axis_size("ctx")
    own = width // n
    tokens_all = tok * n
    table = jnp.transpose(bias_table)
    pad = jnp.zeros((12 * CHUNK - width,), F32)
    rest = jnp.zeros((5 * CHUNK,), F32)
    params = jnp.concatenate(
        [norm_attn, pad, norm_ffn, pad, delete_mask.astype(F32), rest]
    ).reshape(32, CHUNK)
    xt = jnp.transpose(inputs)
    ogt = jnp.transpose(out_grad)
    wq = jnp.transpose(w_query)
    wk = jnp.transpose(w_key)
    wv = jnp.transpose(w_value)
    q, kv, masks, lse, pair, mid, two, og, lhs_two, lhs_og, lhs_one, square = front(
        xt, ogt, wq, wk, wv, w_output, table, params
    )
    down, gate, up, tail, y, dx, small = back(
        (
            two,
            og,
            mid,
            params,
            q,
            lse,
            pair,
            w_output,
            wq,
            wk,
            wv,
            masks,
            table,
            square,
            w_gate,
            w_up,
            jnp.transpose(w_down),
            lhs_two,
            lhs_og,
            lhs_one,
            kv,
            ogt,
            xt,
        ),
        own,
    )
    down, gate, up, y, dx, masked, query, key, value, output, table, one, two, root = finish(
        small, tail, dealing.reshape(tokens_all // CHUNK, CHUNK), own, (down, gate, up), (y, dx)
    )
    return (
        jnp.transpose(y),
        jnp.transpose(dx),
        masked.reshape(tok),
        query,
        key,
        value,
        output,
        jnp.transpose(table),
        one.reshape(own),
        gate,
        up,
        jnp.transpose(down),
        two.reshape(own),
        root.reshape(3),
    )


def local(inputs, delete_mask, lengths, *rest):
    tok = inputs.shape[0]
    fits = lax.axis_size("ctx") == 16 and lax.axis_size("wt") == 2 and tok == 3 * CHUNK
    fits = fits and tok * 16 == MIN_LEN * lengths.shape[0] and inputs.shape[1] == 1472
    fits = fits and rest[1].shape[1] == 3 * HD and rest[7].shape[1] == GROUPS * TILE
    return (even if fits else general)(inputs, delete_mask, lengths, *rest)


def solution(mesh):
    return jax.shard_map(
        local,
        mesh=mesh,
        in_specs=(
            P("ctx", None),
            P("ctx"),
            P(),
            P(),
            P(None, "wt"),
            P(None, "wt"),
            P(None, "wt"),
            P("wt", None),
            P(None, "wt"),
            P(),
            P(None, "wt"),
            P(None, "wt"),
            P("wt", None),
            P(),
            P("ctx", None),
        ),
        out_specs=(
            P("ctx", None),
            P("ctx", None),
            P("ctx"),
            P("ctx", "wt"),
            P("ctx", "wt"),
            P("ctx", "wt"),
            P("wt", "ctx"),
            P(None, "wt"),
            P("ctx"),
            P("ctx", "wt"),
            P("ctx", "wt"),
            P("wt", "ctx"),
            P("ctx"),
            P(),
        ),
        check_vma=False,
    )
```
